32 devices in a mesh: dp: 8 (over z, x), mp: 4 (over y, core).
Axes of the slice: x: 2, y: 2, z: 4, core: 2. Of those that a mesh axis runs over, the one named last changes fastest.
Arguments:
- out_grads: bfloat16 [2048, 8192], P('dp'), may hold values from -6 to 6
- hidden_acts: bfloat16 [2048, 28672], P('dp', 'mp'), may hold values from -6 to 6
- out_basis: bfloat16 [16, 512, 512], P('mp'), may hold values from -0.25 to 0.25
- in_basis: bfloat16 [112, 256, 256], P('mp'), may hold values from -0.375 to 0.375
- left_store: bfloat16 [8, 512, 8192], P('dp', None, 'mp'), may hold values from -0.0625 to 0.0625
- right_store: bfloat16 [8, 512, 28672], P('dp', None, 'mp'), may hold values from -0.03125 to 0.03125
- owners: int32 [16], replicated, may hold values from 0 to 7, as said below
Outputs:
- scores: float32 [16, 16], P('dp')
The draws below stay inside these ranges and needn't reach their ends.
Inputs may be any that keep to these rules, and one draw needn't show every extreme that they name: `owners`: every group index is the owner of exactly 16 // 8 queries.
All inputs are finite; a program needn't handle non-finite values.
Results may differ from the reference program's by a relative error of at most 0.0003.
Values may be sent and summed in bfloat16 or wider, within the bound.
No kernel may reach another device: no remote copies, remote signals or barrier semaphores. Data moves between devices by JAX's collectives and lax.ppermute only.
A program may use at most 128 MiB of HBM per device.

```python
import jax
import jax.numpy as jnp
from jax import lax

D = 8192
FF = 28672
BS = 512
BA = 256
NQ = 16
R = 32
LEN = 128
TOKENS = 2048
N_DP = 8


def draw_owners(key, part):
    key = jax.random.fold_in(key, 7)
    shuffled = jax.random.permutation(key, N_DP).astype(jnp.int32)
    return jnp.tile(shuffled, NQ // N_DP)


def levels(key, dims, split, least, largest):
    factor_of = 1.0
    for axis_at, shards_of in split:
        draws = jax.random.uniform(jax.random.fold_in(jax.random.fold_in(key, 6), axis_at), (shards_of,), jnp.float32, least / len(split), largest / len(split))
        factor_of = factor_of * jnp.repeat(jnp.exp(draws), dims[axis_at] // shards_of).reshape((-1,) + (1,) * (len(dims) - 1 - axis_at))
    return factor_of


def noise(stream_key, dims, width, reach, cuts=(), kind=jnp.bfloat16):
    drawn = width * jax.random.normal(stream_key, dims, jnp.float32)
    if cuts:
        drawn = drawn * levels(stream_key, dims, cuts, -0.22, 0.18)
    return jnp.clip(drawn, -reach, reach).astype(kind)


def setup_inputs(seed: int = 0) -> dict:
    splits = jax.random.split(jax.random.key(seed), 8)
    out_grads = noise(splits[0], (TOKENS, D), 1.0, 6.0, ((0, 8),))
    hidden_acts = noise(splits[1], (TOKENS, FF), 1.0, 6.0, ((0, 8), (1, 4)))
    out_basis = noise(splits[2], (D // BS, BS, BS), BS ** -0.5, 0.25, ((0, 4),))
    in_basis = noise(splits[3], (FF // BA, BA, BA), BA ** -0.5, 0.375, ((0, 4),))
    left_store = noise(splits[4], (N_DP, NQ * R, D), D ** -0.5, 0.0625, ((0, 8), (2, 4)))
    right_store = noise(splits[5], (N_DP, NQ * R, FF), FF ** -0.5, 0.03125, ((0, 8), (2, 4)))
    owners = draw_owners(jax.random.fold_in(splits[7], 71), 0)
    return dict(out_grads=out_grads, hidden_acts=hidden_acts, out_basis=out_basis, in_basis=in_basis, left_store=left_store, right_store=right_store, owners=owners)


def pick_factors(factor_store, owners):
    columns = jnp.repeat(owners, R)
    chosen = columns[None, :] == jnp.arange(factor_store.shape[0], dtype=jnp.int32)[:, None]
    return jnp.sum(jnp.where(chosen[:, :, None], factor_store.astype(jnp.float32), jnp.float32(0.0)), axis=0)


def rotate(matrix_rows, eigenbasis, block_width):
    blocks = matrix_rows.astype(jnp.float32).reshape(matrix_rows.shape[0], -1, block_width)
    turned = jnp.einsum("tbi,bij->tbj", blocks, eigenbasis.astype(jnp.float32), precision=lax.Precision.HIGHEST)
    return turned.reshape(matrix_rows.shape[0], -1)


def reference(out_grads, hidden_acts, out_basis, in_basis, left_store, right_store, owners):
    left = pick_factors(left_store, owners)
    right = pick_factors(right_store, owners)

    def per_sequence(sequence_pair):
        grad_rows, act_rows = sequence_pair
        contract = (((1,), (1,)), ((), ()))
        coefficient = lax.dot_general(rotate(grad_rows, out_basis, BS), left, contract, precision=lax.Precision.HIGHEST)
        projected = lax.dot_general(rotate(act_rows, in_basis, BA), right, contract, precision=lax.Precision.HIGHEST)
        return jnp.sum((coefficient * projected).reshape(LEN, NQ, R), axis=(0, 2)) / jnp.float32(LEN)

    return lax.map(per_sequence, (out_grads.reshape(-1, LEN, D), hidden_acts.reshape(-1, LEN, FF)))
```

```python
import jax
import jax.numpy as jnp
from jax import lax
from jax.sharding import PartitionSpec as P

NQ = 16
R = 32
LEN = 128


def block_rotate(matrix_rows, eigenbasis):
    block_width = eigenbasis.shape[1]
    blocks = matrix_rows.reshape(matrix_rows.shape[0], -1, block_width)
    turned = jnp.einsum("tbi,bij->tbj", blocks, eigenbasis, preferred_element_type=jnp.float32)
    return turned.reshape(matrix_rows.shape[0], -1)


def contract_rows(first, second):
    high = lax.reduce_precision(first, 8, 7)
    low = (first - high).astype(jnp.bfloat16)
    rows = first.shape[0]
    both = jnp.concatenate([high.astype(jnp.bfloat16), low], axis=0)
    out = lax.dot_general(
        both, second, (((1,), (1,)), ((), ())), preferred_element_type=jnp.float32
    )
    return out[:rows] + out[rows:]


def ranks(owners):
    at = jnp.arange(NQ, dtype=jnp.int32)
    before = (owners[None, :] < owners[:, None]) | (
        (owners[None, :] == owners[:, None]) & (at[None, :] < at[:, None])
    )
    place = jnp.sum(before.astype(jnp.int32), axis=1)
    order = jnp.sum(jnp.where(place[None, :] == at[:, None], at[None, :], 0), axis=1)
    return place, order


def on_device(groups, out_grads, hidden_acts, out_basis, in_basis, left_store, right_store, owners):
    per = NQ // groups
    group = lax.axis_index("dp")
    shard = lax.axis_index("mp")
    place, order = ranks(owners)

    def own_rows(store):
        return jnp.concatenate(
            [
                lax.dynamic_slice_in_dim(store[0], order[group * per + i] * R, R, 0)
                for i in range(per)
            ],
            axis=0,
        )

    left_fac = lax.all_gather(own_rows(left_store), "dp", axis=0, tiled=True)
    right_fac = lax.all_gather(own_rows(right_store), "dp", axis=0, tiled=True)

    width_left = left_store.shape[2]
    grads = lax.dynamic_slice_in_dim(out_grads, shard * width_left, width_left, 1)
    coefficient = lax.psum(contract_rows(block_rotate(grads, out_basis), left_fac), "mp")
    projected = contract_rows(block_rotate(hidden_acts, in_basis), right_fac)
    per_sequence = jnp.sum(
        (coefficient * projected).reshape(-1, LEN, NQ, R), axis=(1, 3)
    ) / jnp.float32(LEN)
    scores = lax.psum(per_sequence, "mp")
    at = jnp.arange(NQ, dtype=jnp.int32)
    return jnp.sum(jnp.where(place[None, None, :] == at[None, :, None], scores[:, :, None], 0.0), axis=1)


def solution(mesh):
    in_specs = (
        P("dp", None),
        P("dp", "mp"),
        P("mp", None, None),
        P("mp", None, None),
        P("dp", None, "mp"),
        P("dp", None, "mp"),
        P(),
    )
    out_specs = P("dp", None)
    groups = mesh.shape["dp"]

    def whole(*arrays):
        return on_device(groups, *arrays)

    return jax.shard_map(whole, mesh=mesh, in_specs=in_specs, out_specs=out_specs, check_vma=False)
```

```python
import jax
import jax.numpy as jnp
from jax import lax
from jax.sharding import Mesh, PartitionSpec as P

NQ = 16
R = 32
LEN = 128


def block_rotate(matrix_rows, eigenbasis):
    block_width = eigenbasis.shape[1]
    blocks = matrix_rows.reshape(matrix_rows.shape[0], -1, block_width)
    turned = jnp.einsum("tbi,bij->tbj", blocks, eigenbasis, preferred_element_type=jnp.float32)
    return turned.reshape(matrix_rows.shape[0], -1)


def two_terms(first):
    high = lax.reduce_precision(first, 8, 7)
    low = (first - high).astype(jnp.bfloat16)
    return jnp.concatenate([high.astype(jnp.bfloat16), low], axis=0)


def contract_rows(both, second):
    rows = both.shape[0] // 2
    out = lax.dot_general(
        both, second, (((1,), (1,)), ((), ())), preferred_element_type=jnp.float32
    )
    return out[:rows] + out[rows:]


def ranks(owners):
    at = jnp.arange(NQ, dtype=jnp.int32)
    before = (owners[None, :] < owners[:, None]) | (
        (owners[None, :] == owners[:, None]) & (at[None, :] < at[:, None])
    )
    place = jnp.sum(before.astype(jnp.int32), axis=1)
    order = jnp.sum(jnp.where(place[None, :] == at[:, None], at[None, :], 0), axis=1)
    return place, order


def by_query(scores, column_of):
    at = jnp.arange(NQ, dtype=jnp.int32)
    return jnp.sum(
        jnp.where(column_of[None, None, :] == at[None, :, None], scores[:, :, None], 0.0), axis=1
    )


def whole_width(groups, out_grads, hidden_acts, out_basis, in_basis, left_store, right_store, owners):
    per = NQ // groups
    group = lax.axis_index("dp")
    shard = lax.axis_index("mp")
    place, order = ranks(owners)

    def own_rows(store):
        return jnp.concatenate(
            [
                lax.dynamic_slice_in_dim(store[0], order[group * per + i] * R, R, 0)
                for i in range(per)
            ],
            axis=0,
        )

    left_fac = lax.all_gather(own_rows(left_store), "dp", axis=0, tiled=True)
    right_fac = lax.all_gather(own_rows(right_store), "dp", axis=0, tiled=True)
    width_left = left_store.shape[2]
    grads = lax.dynamic_slice_in_dim(out_grads, shard * width_left, width_left, 1)
    coefficient = lax.psum(
        contract_rows(two_terms(block_rotate(grads, out_basis)), left_fac), "mp"
    )
    projected = contract_rows(two_terms(block_rotate(hidden_acts, in_basis)), right_fac)
    per_sequence = jnp.sum(
        (coefficient * projected).reshape(-1, LEN, NQ, R), axis=(1, 3)
    ) / jnp.float32(LEN)
    return by_query(lax.psum(per_sequence, "mp"), place)


def arrivals(count):
    table = []
    for z in range(count):
        got = []
        for hops in range(1, count):
            if z - hops >= 0:
                got.append((0, hops))
            if z + hops < count:
                got.append((1, hops))
        table.append(got)
    return table


def half_width(count, out_grads, hidden_acts, out_basis, in_basis, left_store, right_store, owners):
    per = NQ // (2 * count)
    line = lax.axis_index("hi")
    side = lax.axis_index("lo")
    shard = lax.axis_index("mp")
    place, order = ranks(owners)
    group = line * 2 + side
    tokens = out_grads.shape[0]
    half_left = left_store.shape[2] // 2
    half_right = right_store.shape[2] // 2
    swap = [(0, 1), (1, 0)]

    def own_rows(store, half, which):
        return jnp.concatenate(
            [
                lax.dynamic_slice(
                    store[0], (order[group * per + i] * R, which * half), (R, half)
                )
                for i in range(per)
            ],
            axis=0,
        )

    def along_line(own):
        ups, downs = [own], [own]
        for hops in range(1, count):
            ups.append(lax.ppermute(ups[-1], "hi", [(i, i + 1) for i in range(hops - 1, count - 1)]))
            downs.append(lax.ppermute(downs[-1], "hi", [(i, i - 1) for i in range(1, count - hops + 1)]))
        return ups, downs

    table = arrivals(count)

    def slot(pieces, i):
        if i == 0:
            return pieces[0][0]
        chosen = None
        for z in range(count):
            direction, hops = table[z][i - 1]
            piece = pieces[direction][hops]
            chosen = piece if chosen is None else jnp.where(line == z, piece, chosen)
        return chosen

    def halves(matrix, half, base):
        keep = lax.dynamic_slice_in_dim(matrix, base + side * half, half, 1)
        give = lax.dynamic_slice_in_dim(matrix, base + (1 - side) * half, half, 1)
        return keep, give

    left_own = own_rows(left_store, half_left, side)
    right_own = own_rows(right_store, half_right, side)
    left_other = lax.ppermute(own_rows(left_store, half_left, 1 - side), "lo", swap)
    right_other = lax.ppermute(own_rows(right_store, half_right, 1 - side), "lo", swap)
    grads_keep, grads_give = halves(out_grads, half_left, shard * left_store.shape[2])
    acts_keep, acts_give = halves(hidden_acts, half_right, 0)
    grads_other = lax.ppermute(grads_give, "lo", swap)
    acts_other = lax.ppermute(acts_give, "lo", swap)

    left_line = along_line(left_own)
    left_line_other = along_line(left_other)
    right_line = along_line(right_own)
    right_line_other = along_line(right_other)

    def own_basis(basis):
        blocks = basis.shape[0] // 2
        return lax.dynamic_slice_in_dim(basis, side * blocks, blocks, 0)

    out_half = own_basis(out_basis)
    in_half = own_basis(in_basis)
    grads = two_terms(block_rotate(jnp.concatenate([grads_keep, grads_other], axis=0), out_half))
    acts = two_terms(block_rotate(jnp.concatenate([acts_keep, acts_other], axis=0), in_half))

    left_fac = jnp.concatenate(
        [piece for i in range(count) for piece in (slot(left_line, i), slot(left_line_other, i))], axis=0
    )
    chunk = per * R

    def other_way(matrix):
        turned = matrix.reshape(2, tokens, count, 2, chunk)[::-1, :, :, ::-1]
        return jnp.where(side == 0, matrix, turned.reshape(matrix.shape))

    coefficient = contract_rows(grads, left_fac)
    coefficient = other_way(lax.psum(other_way(coefficient), ("lo", "mp")))

    parts = []
    for i in range(count):
        right_fac = jnp.concatenate([slot(right_line, i), slot(right_line_other, i)], axis=0)
        projected = contract_rows(acts, right_fac)
        terms = coefficient[:, 2 * i * chunk : 2 * (i + 1) * chunk] * projected
        parts.append(jnp.sum(terms.reshape(-1, LEN, 2 * per, R), axis=(1, 3)))
    partial = jnp.concatenate(parts, axis=1) / jnp.float32(LEN)
    sequences = tokens // LEN
    turned = partial.reshape(2, sequences, count, 2, per)[::-1, :, :, ::-1].reshape(partial.shape)
    partial = jnp.where(side == 0, partial, turned)
    scores = lax.psum(partial, ("lo", "mp"))
    scores = lax.dynamic_slice_in_dim(scores, side * sequences, sequences, 0)

    owner_group = place // per
    owner_line = owner_group // 2
    slot_of = []
    for z in range(count):
        places = [0] * count
        for i, (direction, hops) in enumerate(table[z]):
            places[z - hops if direction == 0 else z + hops] = i + 1
        slot_of.append(places)
    slots = jnp.zeros_like(owner_line)
    for z in range(count):
        for source in range(count):
            slots = jnp.where((line == z) & (owner_line == source), slot_of[z][source], slots)
    column_of = (slots * 2 + owner_group % 2) * per + place % per
    return by_query(scores, column_of)


def solution(mesh):
    groups = mesh.shape["dp"]
    shards = mesh.shape["mp"]
    paired = Mesh(mesh.devices.reshape(groups // 2, 2, shards), ("hi", "lo", "mp"))

    def whole(*arrays):
        blocks = [basis.shape[0] // shards for basis in arrays[2:4]]
        if any(count % 2 for count in blocks):
            dp, used = "dp", mesh
            body = lambda *local: whole_width(groups, *local)
        else:
            dp, used = ("hi", "lo"), paired
            body = lambda *local: half_width(groups // 2, *local)
        in_specs = (
            P(dp, None),
            P(dp, "mp"),
            P("mp", None, None),
            P("mp", None, None),
            P(dp, None, "mp"),
            P(dp, None, "mp"),
            P(),
        )
        return jax.shard_map(
            body, mesh=used, in_specs=in_specs, out_specs=P(dp, None), check_vma=False
        )(*arrays)

    return whole
```

```python
import jax
import jax.numpy as jnp
from jax import lax
from jax.experimental import pallas as pl
from jax.experimental.pallas import tpu as pltpu
from jax.sharding import PartitionSpec as P

NQ = 16
R = 32
LEN = 128


def params():
    return pltpu.CompilerParams(vmem_limit_bytes=48 * 2**20)


def pick_rows(groups, owners, left_store, right_store):
    per = NQ // groups
    width_left = left_store.shape[2]
    half = right_store.shape[2] // 2

    def kernel(owners_ref, left_ref, right_ref, left_out, first_out, second_out, sems):
        group = lax.axis_index("dp")
        found = jnp.int32(0)
        queries = [jnp.int32(0)] * per
        for q in range(NQ):
            own = owners_ref[q] == group
            queries = [jnp.where(own & (found == i), q, at) for i, at in enumerate(queries)]
            found = found + own.astype(jnp.int32)
        copies = []
        for i in range(per):
            rows = pl.ds(pl.multiple_of(queries[i] * R, R), R)
            here = pl.ds(i * R, R)
            pairs = [
                (left_ref.at[0, rows, :], left_out.at[here, :]),
                (right_ref.at[0, rows, pl.ds(0, half)], first_out.at[here, :]),
                (right_ref.at[0, rows, pl.ds(half, half)], second_out.at[here, :]),
            ]
            for j, (source, target) in enumerate(pairs):
                copies.append(pltpu.make_async_copy(source, target, sems.at[i, j]))
        for copy in copies:
            copy.start()
        for copy in copies:
            copy.wait()

    shape = lambda width: jax.ShapeDtypeStruct((per * R, width), jnp.bfloat16)
    anywhere = pl.BlockSpec(memory_space=pl.ANY)
    return pl.pallas_call(
        kernel,
        out_shape=(shape(width_left), shape(half), shape(half)),
        in_specs=[pl.BlockSpec(memory_space=pltpu.SMEM), anywhere, anywhere],
        out_specs=(anywhere, anywhere, anywhere),
        scratch_shapes=[pltpu.SemaphoreType.DMA((per, 3))],
        compiler_params=params(),
        name="pick_rows",
    )(owners, left_store, right_store)


def rotate(matrix, basis, shard):
    rows = matrix.shape[0]
    blocks, width = basis.shape[0], basis.shape[1]
    each = max(n for n in range(1, 5) if blocks % n == 0 and n * width <= 1024)
    steps = blocks // each

    def kernel(shard_ref, matrix_ref, basis_ref, out_ref):
        for k in range(each):
            columns = slice(k * width, (k + 1) * width)
            turned = jnp.dot(
                matrix_ref[:, columns], basis_ref[k], preferred_element_type=jnp.float32
            )
            high = turned.astype(jnp.bfloat16)
            out_ref[:rows, columns] = high
            out_ref[rows:, columns] = (turned - high.astype(jnp.float32)).astype(jnp.bfloat16)

    total = blocks * width
    return pl.pallas_call(
        kernel,
        out_shape=jax.ShapeDtypeStruct((2 * rows, total), jnp.bfloat16),
        grid_spec=pltpu.PrefetchScalarGridSpec(
            num_scalar_prefetch=1,
            grid=(steps,),
            in_specs=[
                pl.BlockSpec((rows, each * width), lambda k, at: (0, at[0] * steps + k)),
                pl.BlockSpec((each, width, width), lambda k, at: (k, 0, 0)),
            ],
            out_specs=pl.BlockSpec((2 * rows, each * width), lambda k, at: (0, k)),
        ),
        compiler_params=params(),
        cost_estimate=pl.CostEstimate(
            flops=2 * rows * total * width,
            bytes_accessed=2 * (3 * rows * total + total * width),
            transcendentals=0,
        ),
        name="rotate",
    )(jnp.reshape(shard, (1,)).astype(jnp.int32), matrix, basis)


def contract_rows(both, second):
    rows = both.shape[0] // 2
    out = lax.dot_general(
        both, second, (((1,), (1,)), ((), ())), preferred_element_type=jnp.float32
    )
    return out[:rows] + out[rows:]


def places(owners):
    at = jnp.arange(NQ, dtype=jnp.int32)
    before = (owners[None, :] < owners[:, None]) | (
        (owners[None, :] == owners[:, None]) & (at[None, :] < at[:, None])
    )
    return jnp.sum(before.astype(jnp.int32), axis=1)


def swapped(piece, distance, shards):
    return lax.ppermute(piece, "mp", [(i, i ^ distance) for i in range(shards)])


def small_sum(array, shards):
    distance = 1
    while distance < shards:
        reach = min(4, shards // distance)
        array = sum([swapped(array, distance * k, shards) for k in range(1, reach)], array)
        distance *= reach
    return array


def after(value, others):
    return lax.optimization_barrier((value, others))[0] if others else value


def sum_over_shards(matrix, shards, others):
    others = iter(others)
    shard = lax.axis_index("mp")
    bit = shard % 2
    half = matrix.shape[0] // 2

    mine = lax.dynamic_slice_in_dim(matrix, bit * half, half, 0)
    got = swapped(lax.dynamic_slice_in_dim(matrix, (1 - bit) * half, half, 0), 1, shards)
    mine = mine + after(got, next(others, None))
    distance = 2
    while distance < shards:
        mine = mine + after(swapped(mine, distance, shards), next(others, None))
        distance *= 2
    other = swapped(mine, 1, shards)
    return jnp.where(
        bit == 0, jnp.concatenate([mine, other], axis=0), jnp.concatenate([other, mine], axis=0)
    )


def on_device(groups, shards, out_grads, hidden_acts, out_basis, in_basis, left_store, right_store, owners):
    per = NQ // groups
    group = lax.axis_index("dp")
    shard = lax.axis_index("mp")
    place = places(owners)
    chunk = per * R
    ring = list(range(0, groups, 2)) + list(range(groups - 1, 0, -2))
    forward = [(ring[i], ring[(i + 1) % groups]) for i in range(groups)]
    backward = [(b, a) for a, b in forward]
    reach = groups // 2

    own = pick_rows(groups, owners, left_store, right_store)
    half = own[1].shape[1]

    order = [(0, 1), (1, 1)]
    for hops in range(2, reach + 1):
        order += [(0, hops), (2, hops // 2) if hops % 2 == 0 else (1, hops // 2 + 1)]
    for hops in range(1, reach + 1):
        order += [(piece, hops) for piece in (1, 2) if (piece, hops) not in order]
    steps = [[], [], []]
    came = []
    for piece, hops in order:
        ahead, behind = steps[piece][-1] if hops > 1 else (own[piece], own[piece])
        if hops == reach:
            ahead, behind = ahead[: chunk // 2], behind[chunk // 2 :]
        ahead, behind = after((ahead, behind), came[-3:-1])
        got = (lax.ppermute(ahead, "dp", forward), lax.ppermute(behind, "dp", backward))
        steps[piece].append(got)
        came.append(got)

    grads = rotate(out_grads, out_basis, shard)
    acts = rotate(hidden_acts, in_basis, 0)

    left_fac = jnp.concatenate([own[0]] + [piece for step in steps[0] for piece in step], axis=0)
    coefficient = sum_over_shards(
        contract_rows(grads, left_fac), shards, came[order.index((0, reach)) + 1 :]
    )

    parts = []
    at = 0
    for step in range(reach + 1):
        projected = 0.0
        if step == 0:
            factors = own[1:]
        else:
            factors = lax.optimization_barrier((steps[1][step - 1], steps[2][step - 1]))
            factors = [jnp.concatenate(pair, axis=0) for pair in factors]
        for part, factor in enumerate(factors):
            projected += contract_rows(acts[:, part * half : (part + 1) * half], factor)
        width = projected.shape[1]
        terms = coefficient[:, at : at + width] * projected
        parts.append(jnp.sum(terms.reshape(-1, LEN, width), axis=1))
        at += width
    partial = jnp.concatenate(parts, axis=1) / jnp.float32(LEN)

    def position(index):
        return jnp.where(index % 2 == 0, index // 2, groups - 1 - index // 2)

    here = position(group)
    row = jnp.arange(chunk, dtype=jnp.int32) // R
    sources = [(here + 0 * row, row)]
    for hops in range(1, reach + 1):
        ahead, behind = here - hops + 0 * row, here + hops + 0 * row
        if hops < reach:
            sources += [(ahead, row), (behind, row)]
        else:
            cut = chunk // 2
            sources += [(ahead[:cut], row[:cut]), (behind[cut:], row[cut:])]
    source = jnp.concatenate([s for s, _ in sources]) % groups
    row = jnp.concatenate([r for _, r in sources])
    owner = place // per
    hit = (source[:, None] == position(owner)[None, :]) & (row[:, None] == (place % per)[None, :])
    scores = jnp.sum(jnp.where(hit[None], partial[:, :, None], 0.0), axis=1)
    return small_sum(scores, shards)


def solution(mesh):
    groups = mesh.shape["dp"]
    shards = mesh.shape["mp"]
    in_specs = (
        P("dp", None),
        P("dp", "mp"),
        P("mp", None, None),
        P("mp", None, None),
        P("dp", None, "mp"),
        P("dp", None, "mp"),
        P(),
    )

    def whole(*arrays):
        return on_device(groups, shards, *arrays)

    return jax.shard_map(
        whole, mesh=mesh, in_specs=in_specs, out_specs=P("dp", None), check_vma=False
    )
```

```python
import jax
import jax.numpy as jnp
from jax import lax
from jax.experimental import pallas as pl
from jax.experimental.pallas import tpu as pltpu
from jax.sharding import PartitionSpec as P

NQ = 16
R = 32
LEN = 128


def params():
    return pltpu.CompilerParams(vmem_limit_bytes=48 * 2**20)


def pick_rows(groups, owners, left_store, right_store):
    per = NQ // groups
    width_left = left_store.shape[2]
    width_right = right_store.shape[2]
    cut = max(width_right // 4 // 256 * 256, 128)

    def kernel(owners_ref, left_ref, right_ref, first_out, second_out, sems):
        group = lax.axis_index("dp")
        found = jnp.int32(0)
        queries = [jnp.int32(0)] * per
        for q in range(NQ):
            own = owners_ref[q] == group
            queries = [jnp.where(own & (found == i), q, at) for i, at in enumerate(queries)]
            found = found + own.astype(jnp.int32)
        copies = []
        for i in range(per):
            rows = pl.ds(pl.multiple_of(queries[i] * R, R), R)
            here = pl.ds(i * R, R)
            pairs = [
                (left_ref.at[0, rows, :], first_out.at[here, pl.ds(0, width_left)]),
                (right_ref.at[0, rows, pl.ds(0, cut)], first_out.at[here, pl.ds(width_left, cut)]),
                (right_ref.at[0, rows, pl.ds(cut, width_right - cut)], second_out.at[here, :]),
            ]
            for j, (source, target) in enumerate(pairs):
                copies.append(pltpu.make_async_copy(source, target, sems.at[i, j]))
        for copy in copies:
            copy.start()
        for copy in copies:
            copy.wait()

    shape = lambda width: jax.ShapeDtypeStruct((per * R, width), jnp.bfloat16)
    in_hbm = pl.BlockSpec(memory_space=pltpu.HBM)
    return pl.pallas_call(
        kernel,
        out_shape=(shape(width_left + cut), shape(width_right - cut)),
        in_specs=[pl.BlockSpec(memory_space=pltpu.SMEM), in_hbm, in_hbm],
        out_specs=(in_hbm, in_hbm),
        scratch_shapes=[pltpu.SemaphoreType.DMA((per, 3))],
        compiler_params=params(),
        name="pick_rows",
    )(owners, left_store, right_store)


def rotate(matrix, basis, shard):
    rows = matrix.shape[0]
    blocks, width = basis.shape[0], basis.shape[1]
    each = max(n for n in range(1, 5) if blocks % n == 0 and n * width <= 1024)
    steps = blocks // each

    def kernel(shard_ref, matrix_ref, basis_ref, out_ref):
        for k in range(each):
            columns = slice(k * width, (k + 1) * width)
            turned = jnp.dot(
                matrix_ref[:, columns], basis_ref[k], preferred_element_type=jnp.float32
            )
            high = turned.astype(jnp.bfloat16)
            out_ref[:rows, columns] = high
            out_ref[rows:, columns] = (turned - high.astype(jnp.float32)).astype(jnp.bfloat16)

    total = blocks * width
    return pl.pallas_call(
        kernel,
        out_shape=jax.ShapeDtypeStruct((2 * rows, total), jnp.bfloat16),
        grid_spec=pltpu.PrefetchScalarGridSpec(
            num_scalar_prefetch=1,
            grid=(steps,),
            in_specs=[
                pl.BlockSpec((rows, each * width), lambda k, at: (0, at[0] * steps + k)),
                pl.BlockSpec((each, width, width), lambda k, at: (k, 0, 0)),
            ],
            out_specs=pl.BlockSpec((2 * rows, each * width), lambda k, at: (0, k)),
        ),
        compiler_params=params(),
        cost_estimate=pl.CostEstimate(
            flops=2 * rows * total * width,
            bytes_accessed=2 * (3 * rows * total + total * width),
            transcendentals=0,
        ),
        name="rotate",
    )(jnp.reshape(shard, (1,)).astype(jnp.int32), matrix, basis)


def contract_rows(both, second):
    rows = both.shape[0] // 2
    out = lax.dot_general(
        both, second, (((1,), (1,)), ((), ())), preferred_element_type=jnp.float32
    )
    return out[:rows] + out[rows:]


def places(owners):
    at = jnp.arange(NQ, dtype=jnp.int32)
    before = (owners[None, :] < owners[:, None]) | (
        (owners[None, :] == owners[:, None]) & (at[None, :] < at[:, None])
    )
    return jnp.sum(before.astype(jnp.int32), axis=1)


def swapped(piece, distance, shards):
    return lax.ppermute(piece, "mp", [(i, i ^ distance) for i in range(shards)])


def small_sum(array, shards):
    distance = 1
    while distance < shards:
        reach = min(4, shards // distance)
        array = sum([swapped(array, distance * k, shards) for k in range(1, reach)], array)
        distance *= reach
    return array


def after(value, others):
    return lax.optimization_barrier((value, others))[0] if others else value


def sum_over_shards(matrix, shards, others):
    others = iter(others)
    shard = lax.axis_index("mp")
    bit = shard % 2
    half = matrix.shape[0] // 2

    mine = lax.dynamic_slice_in_dim(matrix, bit * half, half, 0)
    got = swapped(lax.dynamic_slice_in_dim(matrix, (1 - bit) * half, half, 0), 1, shards)
    mine = mine + after(got, next(others, None))
    distance = 2
    while distance < shards:
        mine = mine + after(swapped(mine, distance, shards), next(others, None))
        distance *= 2
    other = swapped(mine, 1, shards)
    return jnp.where(
        bit == 0, jnp.concatenate([mine, other], axis=0), jnp.concatenate([other, mine], axis=0)
    )


def on_device(groups, shards, out_grads, hidden_acts, out_basis, in_basis, left_store, right_store, owners):
    per = NQ // groups
    group = lax.axis_index("dp")
    shard = lax.axis_index("mp")
    place = places(owners)
    chunk = per * R
    ring = list(range(0, groups, 2)) + list(range(groups - 1, 0, -2))
    forward = [(ring[i], ring[(i + 1) % groups]) for i in range(groups)]
    backward = [(b, a) for a, b in forward]
    reach = groups // 2

    own = pick_rows(groups, owners, left_store, right_store)
    width_left = left_store.shape[2]
    cut = own[0].shape[1] - width_left

    across = lax.ppermute(
        own[0][:, :width_left], "dp", [(ring[i], ring[i - reach]) for i in range(groups)]
    )
    steps = [[], []]
    came = []
    for hops in range(1, reach + 1):
        for piece in range(2):
            ahead, behind = steps[piece][-1] if hops > 1 else (own[piece], own[piece])
            if hops == reach:
                base = width_left if piece == 0 else 0
                ahead, behind = ahead[: chunk // 2, base:], behind[chunk // 2 :, base:]
            ahead, behind = after((ahead, behind), came[-3:-1])
            got = (lax.ppermute(ahead, "dp", forward), lax.ppermute(behind, "dp", backward))
            steps[piece].append(got)
            came.append(got)

    grads = rotate(out_grads, out_basis, shard)
    acts = rotate(hidden_acts, in_basis, 0)

    steps[0][-1], steps[1][-1] = lax.optimization_barrier((steps[0][-1], steps[1][-1]))
    first = [own[0]] + [jnp.concatenate(pair, axis=0) for pair in steps[0]]
    second = [own[1]] + [jnp.concatenate(pair, axis=0) for pair in steps[1]]
    left_fac = [piece[:, :width_left] for piece in first[:-1]] + [across]
    coefficient = sum_over_shards(
        contract_rows(grads, jnp.concatenate(left_fac, axis=0)), shards, [came[-3]]
    )

    parts = []
    at = 0
    for step in range(reach + 1):
        projected = contract_rows(acts[:, :cut], first[step][:, -cut:])
        projected += contract_rows(acts[:, cut:], second[step])
        width = projected.shape[1]
        terms = coefficient[:, at : at + width] * projected
        parts.append(jnp.sum(terms.reshape(-1, LEN, width), axis=1))
        at += width
    partial = jnp.concatenate(parts, axis=1) / jnp.float32(LEN)

    def position(index):
        return jnp.where(index % 2 == 0, index // 2, groups - 1 - index // 2)

    here = position(group)
    row = jnp.arange(chunk, dtype=jnp.int32) // R
    sources = [(here + 0 * row, row)]
    for hops in range(1, reach + 1):
        ahead, behind = here - hops + 0 * row, here + hops + 0 * row
        if hops < reach:
            sources += [(ahead, row), (behind, row)]
        else:
            cut = chunk // 2
            sources += [(ahead[:cut], row[:cut]), (behind[cut:], row[cut:])]
    source = jnp.concatenate([s for s, _ in sources]) % groups
    row = jnp.concatenate([r for _, r in sources])
    owner = place // per
    hit = (source[:, None] == position(owner)[None, :]) & (row[:, None] == (place % per)[None, :])
    scores = jnp.sum(jnp.where(hit[None], partial[:, :, None], 0.0), axis=1)
    return small_sum(scores, shards)


def solution(mesh):
    groups = mesh.shape["dp"]
    shards = mesh.shape["mp"]
    in_specs = (
        P("dp", None),
        P("dp", "mp"),
        P("mp", None, None),
        P("mp", None, None),
        P("dp", None, "mp"),
        P("dp", None, "mp"),
        P(),
    )

    def whole(*arrays):
        return on_device(groups, shards, *arrays)

    return jax.shard_map(
        whole, mesh=mesh, in_specs=in_specs, out_specs=P("dp", None), check_vma=False
    )
```

```python
import jax
import jax.numpy as jnp
from jax import lax
from jax.experimental import pallas as pl
from jax.experimental.pallas import tpu as pltpu
from jax.sharding import PartitionSpec as P

NQ = 16
R = 32
LEN = 128


def params(mebibytes):
    return pltpu.CompilerParams(vmem_limit_bytes=mebibytes * 2**20)


def pick_rows(groups, owners, left_store, right_store):
    per = NQ // groups
    width_left = left_store.shape[2]
    width_right = right_store.shape[2]
    cut = max(width_right * 5 // 14 // 128 * 128, 128)

    def kernel(owners_ref, left_ref, right_ref, left_out, first_out, second_out, sems):
        group = lax.axis_index("dp")
        found = jnp.int32(0)
        queries = [jnp.int32(0)] * per
        for q in range(NQ):
            own = owners_ref[q] == group
            queries = [jnp.where(own & (found == i), q, at) for i, at in enumerate(queries)]
            found = found + own.astype(jnp.int32)
        copies = []
        for i in range(per):
            rows = pl.ds(pl.multiple_of(queries[i] * R, R), R)
            here = pl.ds(i * R, R)
            pairs = [
                (left_ref.at[0, rows, :], left_out.at[here, :]),
                (right_ref.at[0, rows, pl.ds(0, cut)], first_out.at[here, :]),
                (right_ref.at[0, rows, pl.ds(cut, width_right - cut)], second_out.at[here, :]),
            ]
            for j, (source, target) in enumerate(pairs):
                copies.append(pltpu.make_async_copy(source, target, sems.at[i, j]))
        for copy in copies:
            copy.start()
        for copy in copies:
            copy.wait()

    shape = lambda width: jax.ShapeDtypeStruct((per * R, width), jnp.bfloat16)
    in_hbm = pl.BlockSpec(memory_space=pltpu.HBM)
    return pl.pallas_call(
        kernel,
        out_shape=(shape(width_left), shape(cut), shape(width_right - cut)),
        in_specs=[pl.BlockSpec(memory_space=pltpu.SMEM), in_hbm, in_hbm],
        out_specs=(in_hbm, in_hbm, in_hbm),
        scratch_shapes=[pltpu.SemaphoreType.DMA((per, 3))],
        compiler_params=params(62),
        name="pick_rows",
    )(owners, left_store, right_store)


def rotate(matrix, basis, shard):
    rows = matrix.shape[0]
    blocks, width = basis.shape[0], basis.shape[1]
    each = max(n for n in range(1, 5) if blocks % n == 0 and n * width <= 1024)
    steps = blocks // each

    def kernel(shard_ref, matrix_ref, basis_ref, out_ref):
        for k in range(each):
            columns = slice(k * width, (k + 1) * width)
            turned = jnp.dot(
                matrix_ref[:, columns], basis_ref[k], preferred_element_type=jnp.float32
            )
            high = turned.astype(jnp.bfloat16)
            out_ref[:rows, columns] = high
            out_ref[rows:, columns] = (turned - high.astype(jnp.float32)).astype(jnp.bfloat16)

    total = blocks * width
    return pl.pallas_call(
        kernel,
        out_shape=jax.ShapeDtypeStruct((2 * rows, total), jnp.bfloat16),
        grid_spec=pltpu.PrefetchScalarGridSpec(
            num_scalar_prefetch=1,
            grid=(steps,),
            in_specs=[
                pl.BlockSpec((rows, each * width), lambda k, at: (0, at[0] * steps + k)),
                pl.BlockSpec((each, width, width), lambda k, at: (k, 0, 0)),
            ],
            out_specs=pl.BlockSpec((2 * rows, each * width), lambda k, at: (0, k)),
        ),
        compiler_params=params(56),
        cost_estimate=pl.CostEstimate(
            flops=2 * rows * total * width,
            bytes_accessed=2 * (3 * rows * total + total * width),
            transcendentals=0,
        ),
        name="rotate",
    )(jnp.reshape(shard, (1,)).astype(jnp.int32), matrix, basis)


def contract_rows(both, second):
    rows = both.shape[0] // 2
    out = lax.dot_general(
        both, second, (((1,), (1,)), ((), ())), preferred_element_type=jnp.float32
    )
    return out[:rows] + out[rows:]


def places(owners):
    at = jnp.arange(NQ, dtype=jnp.int32)
    before = (owners[None, :] < owners[:, None]) | (
        (owners[None, :] == owners[:, None]) & (at[None, :] < at[:, None])
    )
    return jnp.sum(before.astype(jnp.int32), axis=1)


def swapped(piece, distance, shards):
    return lax.ppermute(piece, "mp", [(i, i ^ distance) for i in range(shards)])


def small_sum(array, shards):
    distance = 1
    while distance < shards:
        reach = min(4, shards // distance)
        array = sum([swapped(array, distance * k, shards) for k in range(1, reach)], array)
        distance *= reach
    return array


def after(value, others):
    return lax.optimization_barrier((value, others))[0] if others else value


def sum_over_shards(matrix, shards, others):
    others = iter(others)
    shard = lax.axis_index("mp")
    bit = shard % 2
    half = matrix.shape[0] // 2

    mine = lax.dynamic_slice_in_dim(matrix, bit * half, half, 0)
    got = swapped(lax.dynamic_slice_in_dim(matrix, (1 - bit) * half, half, 0), 1, shards)
    mine = mine + after(got, next(others, None))
    distance = 2
    while distance < shards:
        mine = mine + after(swapped(mine, distance, shards), next(others, None))
        distance *= 2
    other = swapped(mine, 1, shards)
    return jnp.where(
        bit == 0, jnp.concatenate([mine, other], axis=0), jnp.concatenate([other, mine], axis=0)
    )


def on_device(groups, shards, out_grads, hidden_acts, out_basis, in_basis, left_store, right_store, owners):
    per = NQ // groups
    group = lax.axis_index("dp")
    shard = lax.axis_index("mp")
    place = places(owners)
    chunk = per * R
    ring = list(range(0, groups, 2)) + list(range(groups - 1, 0, -2))
    forward = [(ring[i], ring[(i + 1) % groups]) for i in range(groups)]
    backward = [(b, a) for a, b in forward]
    reach = groups // 2

    own = pick_rows(groups, owners, left_store, right_store)
    cut = own[1].shape[1]

    def around(piece, before):
        steps = []
        ahead, behind = after((piece, piece), before)
        for hops in range(1, reach + 1):
            if hops == reach:
                ahead, behind = ahead[: chunk // 2], behind[chunk // 2 :]
            ahead = lax.ppermute(ahead, "dp", forward)
            behind = lax.ppermute(behind, "dp", backward)
            steps.append((ahead, behind))
        return steps

    left_steps = around(own[0], None)
    second_steps = around(own[2], None)
    first_steps = around(own[1], left_steps[-1])

    grads = rotate(out_grads, out_basis, shard)
    acts = rotate(hidden_acts, in_basis, 0)

    left_fac = [own[0]] + [piece for pair in left_steps for piece in pair]
    coefficient = sum_over_shards(
        contract_rows(grads, jnp.concatenate(left_fac, axis=0)), shards, []
    )
    first_own, second_own = after(own[1:], left_steps[1])
    first = [first_own] + [jnp.concatenate(pair, axis=0) for pair in first_steps]
    second = [second_own] + [jnp.concatenate(pair, axis=0) for pair in second_steps]

    parts = []
    at = 0
    for step in range(reach + 1):
        projected = contract_rows(acts[:, :cut], first[step])
        projected += contract_rows(acts[:, cut:], second[step])
        width = projected.shape[1]
        terms = coefficient[:, at : at + width] * projected
        parts.append(jnp.sum(terms.reshape(-1, LEN, width), axis=1))
        at += width
    partial = jnp.concatenate(parts, axis=1) / jnp.float32(LEN)

    def position(index):
        return jnp.where(index % 2 == 0, index // 2, groups - 1 - index // 2)

    here = position(group)
    row = jnp.arange(chunk, dtype=jnp.int32) // R
    sources = [(here + 0 * row, row)]
    for hops in range(1, reach + 1):
        ahead, behind = here - hops + 0 * row, here + hops + 0 * row
        if hops < reach:
            sources += [(ahead, row), (behind, row)]
        else:
            cut = chunk // 2
            sources += [(ahead[:cut], row[:cut]), (behind[cut:], row[cut:])]
    source = jnp.concatenate([s for s, _ in sources]) % groups
    row = jnp.concatenate([r for _, r in sources])
    owner = place // per
    hit = (source[:, None] == position(owner)[None, :]) & (row[:, None] == (place % per)[None, :])
    scores = jnp.sum(jnp.where(hit[None], partial[:, :, None], 0.0), axis=1)
    return small_sum(scores, shards)


def solution(mesh):
    groups = mesh.shape["dp"]
    shards = mesh.shape["mp"]
    in_specs = (
        P("dp", None),
        P("dp", "mp"),
        P("mp", None, None),
        P("mp", None, None),
        P("dp", None, "mp"),
        P("dp", None, "mp"),
        P(),
    )

    def whole(*arrays):
        return on_device(groups, shards, *arrays)

    return jax.shard_map(
        whole, mesh=mesh, in_specs=in_specs, out_specs=P("dp", None), check_vma=False
    )
```

```python
import jax
import jax.numpy as jnp
from jax import lax
from jax.experimental import pallas as pl
from jax.experimental.pallas import tpu as pltpu
from jax.sharding import PartitionSpec as P

NQ = 16
R = 32
LEN = 128


def params(mebibytes):
    return pltpu.CompilerParams(vmem_limit_bytes=mebibytes * 2**20)


def pick_rows(groups, owners, left_store, right_store):
    per = NQ // groups
    width_left = left_store.shape[2]
    width_right = right_store.shape[2]
    cut = max(width_right * 5 // 14 // 128 * 128, 128)

    def kernel(owners_ref, left_ref, right_ref, first_out, second_out, sems):
        group = lax.axis_index("dp")
        found = jnp.int32(0)
        queries = [jnp.int32(0)] * per
        for q in range(NQ):
            own = owners_ref[q] == group
            queries = [jnp.where(own & (found == i), q, at) for i, at in enumerate(queries)]
            found = found + own.astype(jnp.int32)
        copies = []
        for i in range(per):
            rows = pl.ds(pl.multiple_of(queries[i] * R, R), R)
            here = pl.ds(i * R, R)
            pairs = [
                (left_ref.at[0, rows, :], first_out.at[here, pl.ds(0, width_left)]),
                (right_ref.at[0, rows, pl.ds(0, cut)], first_out.at[here, pl.ds(width_left, cut)]),
                (right_ref.at[0, rows, pl.ds(cut, width_right - cut)], second_out.at[here, :]),
            ]
            for j, (source, target) in enumerate(pairs):
                copies.append(pltpu.make_async_copy(source, target, sems.at[i, j]))
        for copy in copies:
            copy.start()
        for copy in copies:
            copy.wait()

    shape = lambda width: jax.ShapeDtypeStruct((per * R, width), jnp.bfloat16)
    in_vmem = pl.BlockSpec(memory_space=pltpu.VMEM)
    in_hbm = pl.BlockSpec(memory_space=pltpu.HBM)
    return pl.pallas_call(
        kernel,
        out_shape=(shape(width_left + cut), shape(width_right - cut)),
        in_specs=[pl.BlockSpec(memory_space=pltpu.SMEM), in_hbm, in_hbm],
        out_specs=(in_vmem, in_vmem),
        scratch_shapes=[pltpu.SemaphoreType.DMA((per, 3))],
        compiler_params=params(62),
        name="pick_rows",
    )(owners, left_store, right_store)


def rotate(matrix, basis, shard):
    rows = matrix.shape[0]
    blocks, width = basis.shape[0], basis.shape[1]
    each = max(n for n in range(1, 5) if blocks % n == 0 and n * width <= 1024)
    steps = blocks // each

    def kernel(shard_ref, matrix_ref, basis_ref, out_ref):
        for k in range(each):
            columns = slice(k * width, (k + 1) * width)
            turned = jnp.dot(
                matrix_ref[:, columns], basis_ref[k], preferred_element_type=jnp.float32
            )
            high = turned.astype(jnp.bfloat16)
            out_ref[:rows, columns] = high
            out_ref[rows:, columns] = (turned - high.astype(jnp.float32)).astype(jnp.bfloat16)

    total = blocks * width
    return pl.pallas_call(
        kernel,
        out_shape=jax.ShapeDtypeStruct((2 * rows, total), jnp.bfloat16),
        grid_spec=pltpu.PrefetchScalarGridSpec(
            num_scalar_prefetch=1,
            grid=(steps,),
            in_specs=[
                pl.BlockSpec((rows, each * width), lambda k, at: (0, at[0] * steps + k)),
                pl.BlockSpec((each, width, width), lambda k, at: (k, 0, 0)),
            ],
            out_specs=pl.BlockSpec((2 * rows, each * width), lambda k, at: (0, k)),
        ),
        compiler_params=params(56),
        cost_estimate=pl.CostEstimate(
            flops=2 * rows * total * width,
            bytes_accessed=2 * (3 * rows * total + total * width),
            transcendentals=0,
        ),
        name="rotate",
    )(jnp.reshape(shard, (1,)).astype(jnp.int32), matrix, basis)


def contract_rows(both, second):
    rows = both.shape[0] // 2
    out = lax.dot_general(
        both, second, (((1,), (1,)), ((), ())), preferred_element_type=jnp.float32
    )
    return out[:rows] + out[rows:]


def places(owners):
    at = jnp.arange(NQ, dtype=jnp.int32)
    before = (owners[None, :] < owners[:, None]) | (
        (owners[None, :] == owners[:, None]) & (at[None, :] < at[:, None])
    )
    return jnp.sum(before.astype(jnp.int32), axis=1)


def swapped(piece, distance, shards):
    return lax.ppermute(piece, "mp", [(i, i ^ distance) for i in range(shards)])


def small_sum(array, shards, most):
    distance = 1
    while distance < shards:
        reach = min(most, shards // distance)
        array = sum([swapped(array, distance * k, shards) for k in range(1, reach)], array)
        distance *= reach
    return array


def after(value, others):
    return lax.optimization_barrier((value, others))[0] if others else value


def sum_over_shards(matrix, shards, others):
    others = iter(others)
    shard = lax.axis_index("mp")
    bit = shard % 2
    half = matrix.shape[0] // 2

    mine = lax.dynamic_slice_in_dim(matrix, bit * half, half, 0)
    got = swapped(lax.dynamic_slice_in_dim(matrix, (1 - bit) * half, half, 0), 1, shards)
    mine = mine + after(got, next(others, None))
    distance = 2
    while distance < shards:
        mine = mine + after(swapped(mine, distance, shards), next(others, None))
        distance *= 2
    other = swapped(mine, 1, shards)
    return jnp.where(
        bit == 0, jnp.concatenate([mine, other], axis=0), jnp.concatenate([other, mine], axis=0)
    )


def on_device(groups, shards, out_grads, hidden_acts, out_basis, in_basis, left_store, right_store, owners):
    per = NQ // groups
    group = lax.axis_index("dp")
    shard = lax.axis_index("mp")
    place = places(owners)
    chunk = per * R
    ring = list(range(0, groups, 2)) + list(range(groups - 1, 0, -2))
    forward = [(ring[i], ring[(i + 1) % groups]) for i in range(groups)]
    backward = [(b, a) for a, b in forward]
    reach = groups // 2

    own = pick_rows(groups, owners, left_store, right_store)
    width_left = left_store.shape[2]
    cut = own[0].shape[1] - width_left

    steps = [[], []]
    came = []
    for hops in range(1, reach + 1):
        for piece in range(2):
            ahead, behind = steps[piece][-1] if hops > 1 else (own[piece], own[piece])
            if hops == reach:
                ahead, behind = ahead[: chunk // 2], behind[chunk // 2 :]
            ahead, behind = after((ahead, behind), came[-3:-1])
            got = (lax.ppermute(ahead, "dp", forward), lax.ppermute(behind, "dp", backward))
            steps[piece].append(got)
            came.append(got)

    grads = rotate(out_grads, out_basis, shard)
    acts = rotate(hidden_acts, in_basis, 0)

    steps[0][-1] = after(steps[0][-1], came[-3])
    first_own, second_own = after(own, came[0])
    first = [first_own] + [jnp.concatenate(pair, axis=0) for pair in steps[0]]
    second = [second_own] + [jnp.concatenate(pair, axis=0) for pair in steps[1]]
    left_fac = [piece[:, :width_left] for piece in first]
    coefficient = [
        sum_over_shards(
            contract_rows(grads, jnp.concatenate(left_fac[:-1], axis=0)), shards, [came[-3]]
        ),
        small_sum(contract_rows(grads, left_fac[-1]), shards, 2),
    ]
    coefficient = jnp.concatenate(coefficient, axis=1)

    parts = []
    at = 0
    for step in range(reach + 1):
        projected = contract_rows(acts[:, :cut], first[step][:, width_left:])
        projected += contract_rows(acts[:, cut:], second[step])
        width = projected.shape[1]
        terms = coefficient[:, at : at + width] * projected
        parts.append(jnp.sum(terms.reshape(-1, LEN, width), axis=1))
        at += width
    partial = jnp.concatenate(parts, axis=1) / jnp.float32(LEN)

    def position(index):
        return jnp.where(index % 2 == 0, index // 2, groups - 1 - index // 2)

    here = position(group)
    row = jnp.arange(chunk, dtype=jnp.int32) // R
    sources = [(here + 0 * row, row)]
    for hops in range(1, reach + 1):
        ahead, behind = here - hops + 0 * row, here + hops + 0 * row
        if hops < reach:
            sources += [(ahead, row), (behind, row)]
        else:
            cut = chunk // 2
            sources += [(ahead[:cut], row[:cut]), (behind[cut:], row[cut:])]
    source = jnp.concatenate([s for s, _ in sources]) % groups
    row = jnp.concatenate([r for _, r in sources])
    owner = place // per
    hit = (source[:, None] == position(owner)[None, :]) & (row[:, None] == (place % per)[None, :])
    scores = jnp.sum(jnp.where(hit[None], partial[:, :, None], 0.0), axis=1)
    return small_sum(scores, shards, 4)


def solution(mesh):
    groups = mesh.shape["dp"]
    shards = mesh.shape["mp"]
    in_specs = (
        P("dp", None),
        P("dp", "mp"),
        P("mp", None, None),
        P("mp", None, None),
        P("dp", None, "mp"),
        P("dp", None, "mp"),
        P(),
    )

    def whole(*arrays):
        return on_device(groups, shards, *arrays)

    return jax.shard_map(
        whole, mesh=mesh, in_specs=in_specs, out_specs=P("dp", None), check_vma=False
    )
```

```python
import jax
import jax.numpy as jnp
from jax import lax
from jax.experimental import pallas as pl
from jax.experimental.pallas import tpu as pltpu
from jax.sharding import PartitionSpec as P

NQ = 16
R = 32
LEN = 128


def params(mebibytes):
    return pltpu.CompilerParams(vmem_limit_bytes=mebibytes * 2**20)


def pick_rows(groups, owners, left_store, right_store):
    per = NQ // groups
    width_left = left_store.shape[2]
    width_right = right_store.shape[2]
    cut = max(width_right * 5 // 14 // 128 * 128, 128)

    def kernel(owners_ref, left_ref, right_ref, first_out, second_out, sems):
        group = lax.axis_index("dp")
        found = jnp.int32(0)
        queries = [jnp.int32(0)] * per
        for q in range(NQ):
            own = owners_ref[q] == group
            queries = [jnp.where(own & (found == i), q, at) for i, at in enumerate(queries)]
            found = found + own.astype(jnp.int32)
        copies = []
        for i in range(per):
            rows = pl.ds(pl.multiple_of(queries[i] * R, R), R)
            here = pl.ds(i * R, R)
            pairs = [
                (left_ref.at[0, rows, :], first_out.at[here, pl.ds(0, width_left)]),
                (right_ref.at[0, rows, pl.ds(0, cut)], first_out.at[here, pl.ds(width_left, cut)]),
                (right_ref.at[0, rows, pl.ds(cut, width_right - cut)], second_out.at[here, :]),
            ]
            for j, (source, target) in enumerate(pairs):
                copies.append(pltpu.make_async_copy(source, target, sems.at[i, j]))
        for copy in copies:
            copy.start()
        for copy in copies:
            copy.wait()

    shape = lambda width: jax.ShapeDtypeStruct((per * R, width), jnp.bfloat16)
    in_vmem = pl.BlockSpec(memory_space=pltpu.VMEM)
    in_hbm = pl.BlockSpec(memory_space=pltpu.HBM)
    return pl.pallas_call(
        kernel,
        out_shape=(shape(width_left + cut), shape(width_right - cut)),
        in_specs=[pl.BlockSpec(memory_space=pltpu.SMEM), in_hbm, in_hbm],
        out_specs=(in_vmem, in_vmem),
        scratch_shapes=[pltpu.SemaphoreType.DMA((per, 3))],
        compiler_params=params(62),
        name="pick_rows",
    )(owners, left_store, right_store)


def rotate(matrix, basis, shard):
    rows = matrix.shape[0]
    blocks, width = basis.shape[0], basis.shape[1]
    each = max(n for n in range(1, 5) if blocks % n == 0 and n * width <= 1024)
    steps = blocks // each

    def kernel(shard_ref, matrix_ref, basis_ref, out_ref):
        for k in range(each):
            columns = slice(k * width, (k + 1) * width)
            turned = jnp.dot(
                matrix_ref[:, columns], basis_ref[k], preferred_element_type=jnp.float32
            )
            high = turned.astype(jnp.bfloat16)
            out_ref[:rows, columns] = high
            out_ref[rows:, columns] = (turned - high.astype(jnp.float32)).astype(jnp.bfloat16)

    total = blocks * width
    return pl.pallas_call(
        kernel,
        out_shape=jax.ShapeDtypeStruct((2 * rows, total), jnp.bfloat16),
        grid_spec=pltpu.PrefetchScalarGridSpec(
            num_scalar_prefetch=1,
            grid=(steps,),
            in_specs=[
                pl.BlockSpec((rows, each * width), lambda k, at: (0, at[0] * steps + k)),
                pl.BlockSpec((each, width, width), lambda k, at: (k, 0, 0)),
            ],
            out_specs=pl.BlockSpec((2 * rows, each * width), lambda k, at: (0, k)),
        ),
        compiler_params=params(56),
        cost_estimate=pl.CostEstimate(
            flops=2 * rows * total * width,
            bytes_accessed=2 * (3 * rows * total + total * width),
            transcendentals=0,
        ),
        name="rotate",
    )(jnp.reshape(shard, (1,)).astype(jnp.int32), matrix, basis)


def contract_rows(both, second):
    rows = both.shape[0] // 2
    out = lax.dot_general(
        both, second, (((1,), (1,)), ((), ())), preferred_element_type=jnp.float32
    )
    return out[:rows] + out[rows:]


def score(coefficients, projected, hit):
    sequences = coefficients[0].shape[0] // LEN
    count = len(coefficients)

    def kernel(hit_ref, *refs):
        out = jnp.zeros((sequences, NQ), jnp.float32)
        at = 0
        which, base = 0, 0
        for part_ref in refs[count:-1]:
            width = part_ref.shape[1]
            if base == refs[which].shape[1]:
                which, base = which + 1, 0
            terms = refs[which][:, base : base + width] * part_ref[...]
            base += width
            out += jnp.dot(
                jnp.sum(terms.reshape(sequences, LEN, width), axis=1) * (1.0 / LEN),
                hit_ref[at : at + width, :],
                precision=lax.Precision.HIGHEST,
                preferred_element_type=jnp.float32,
            )
            at += width
        refs[-1][...] = out

    return pl.pallas_call(
        kernel,
        out_shape=jax.ShapeDtypeStruct((sequences, NQ), jnp.float32),
        compiler_params=params(32),
        name="score",
    )(hit, *coefficients, *projected)


def places(owners):
    at = jnp.arange(NQ, dtype=jnp.int32)
    before = (owners[None, :] < owners[:, None]) | (
        (owners[None, :] == owners[:, None]) & (at[None, :] < at[:, None])
    )
    return jnp.sum(before.astype(jnp.int32), axis=1)


def swapped(piece, distance, shards):
    return lax.ppermute(piece, "mp", [(i, i ^ distance) for i in range(shards)])


def small_sum(array, shards, most, distance=1):
    while distance < shards:
        reach = min(most, shards // distance)
        array = sum([swapped(array, distance * k, shards) for k in range(1, reach)], array)
        distance *= reach
    return array


def after(value, others):
    return lax.optimization_barrier((value, others))[0] if jax.tree.leaves(others) else value


def sum_over_shards(matrix, shards):
    shard = lax.axis_index("mp")
    bit = shard % 2
    half = matrix.shape[0] // 2
    mine = lax.dynamic_slice_in_dim(matrix, bit * half, half, 0)
    mine = mine + swapped(lax.dynamic_slice_in_dim(matrix, (1 - bit) * half, half, 0), 1, shards)
    mine = small_sum(mine, shards, 2, 2)
    other = swapped(mine, 1, shards)
    return jnp.where(
        bit == 0, jnp.concatenate([mine, other], axis=0), jnp.concatenate([other, mine], axis=0)
    )


def on_device(groups, shards, out_grads, hidden_acts, out_basis, in_basis, left_store, right_store, owners):
    per = NQ // groups
    group = lax.axis_index("dp")
    shard = lax.axis_index("mp")
    place = places(owners)
    chunk = per * R
    ring = list(range(0, groups, 2)) + list(range(groups - 1, 0, -2))
    forward = [(ring[i], ring[(i + 1) % groups]) for i in range(groups)]
    backward = [(b, a) for a, b in forward]
    reach = groups // 2

    own = pick_rows(groups, owners, left_store, right_store)
    width_left = left_store.shape[2]
    cut = own[0].shape[1] - width_left

    steps = [[], []]
    came = []

    def send(piece, hops, others):
        ahead, behind = steps[piece][-1] if hops > 1 else (own[piece], own[piece])
        if hops == reach:
            ahead, behind = ahead[: chunk // 2], behind[chunk // 2 :]
        ahead, behind = after((ahead, behind), others)
        got = (lax.ppermute(ahead, "dp", forward), lax.ppermute(behind, "dp", backward))
        steps[piece].append(got)
        came.append(got)

    def side_by_side(step):
        return jnp.concatenate(step, axis=0)

    grads = rotate(out_grads, out_basis, shard)
    acts = rotate(hidden_acts, in_basis, 0)

    for hops in range(1, reach):
        send(0, hops, came[-3:-1])
        send(1, hops, came[-3:-1])
    own_later = after(own, came[0])
    first = [side_by_side(step) for step in steps[0][:-1]] + [own_later[0]]
    second = [side_by_side(step) for step in steps[1][:-1]] + [own_later[1]]
    left_fac = jnp.concatenate([part[:, :width_left] for part in first], axis=0)
    coefficients = [sum_over_shards(contract_rows(grads, left_fac), shards)]
    send(0, reach, came[-3:-1] + coefficients)

    first.append(side_by_side(steps[0][reach - 2]))
    part = contract_rows(grads, first[-1][:, :width_left])
    coefficients.append(small_sum(part, shards, 2))
    send(1, reach, came[-3:-1])

    last = after(steps[0][-1], came[-3])
    second.append(side_by_side(after(steps[1][reach - 2], last)))
    first.append(side_by_side(last))
    part = contract_rows(grads, first[-1][:, :width_left])
    part = part + swapped(part, 1, shards)
    second.append(side_by_side(after(steps[1][-1], part)))
    coefficients.append(small_sum(part, shards, 2, 2))

    projected = [
        contract_rows(acts[:, :cut], one[:, width_left:]) + contract_rows(acts[:, cut:], other)
        for one, other in zip(first, second)
    ]

    def position(index):
        return jnp.where(index % 2 == 0, index // 2, groups - 1 - index // 2)

    here = position(group)
    row = jnp.arange(chunk, dtype=jnp.int32) // R
    sources = []
    for hops in range(1, reach):
        if hops == reach - 1:
            sources.append((here + 0 * row, row))
        sources += [(here - hops + 0 * row, row), (here + hops + 0 * row, row)]
    half = chunk // 2
    sources += [(here - reach + 0 * row[:half], row[:half]), (here + reach + 0 * row[half:], row[half:])]
    source = jnp.concatenate([s for s, _ in sources]) % groups
    row = jnp.concatenate([r for _, r in sources])
    owner = place // per
    hit = (source[:, None] == position(owner)[None, :]) & (row[:, None] == (place % per)[None, :])
    scores = score(coefficients, projected, hit.astype(jnp.float32))
    return small_sum(scores, shards, 4)


def solution(mesh):
    groups = mesh.shape["dp"]
    shards = mesh.shape["mp"]
    in_specs = (
        P("dp", None),
        P("dp", "mp"),
        P("mp", None, None),
        P("mp", None, None),
        P("dp", None, "mp"),
        P("dp", None, "mp"),
        P(),
    )

    def whole(*arrays):
        return on_device(groups, shards, *arrays)

    return jax.shard_map(
        whole, mesh=mesh, in_specs=in_specs, out_specs=P("dp", None), check_vma=False
    )
```

```python
import jax
import jax.numpy as jnp
from jax import lax
from jax.experimental import pallas as pl
from jax.experimental.pallas import tpu as pltpu
from jax.sharding import PartitionSpec as P

NQ = 16
R = 32
LEN = 128


def params(mebibytes):
    return pltpu.CompilerParams(vmem_limit_bytes=mebibytes * 2**20)


def pick_rows(groups, owners, parts):
    per = NQ // groups
    total = sum(width for _, _, width in parts)

    def kernel(owners_ref, *refs):
        stores, out_ref, sems = refs[:-2], refs[-2], refs[-1]
        group = lax.axis_index("dp")
        found = jnp.int32(0)
        queries = [jnp.int32(0)] * per
        for q in range(NQ):
            own = owners_ref[q] == group
            queries = [jnp.where(own & (found == i), q, at) for i, at in enumerate(queries)]
            found = found + own.astype(jnp.int32)
        copies = []
        for i in range(per):
            rows = pl.ds(pl.multiple_of(queries[i] * R, R), R)
            at = 0
            for j, (store_ref, (_, base, width)) in enumerate(zip(stores, parts)):
                copies.append(
                    pltpu.make_async_copy(
                        store_ref.at[0, rows, pl.ds(base, width)],
                        out_ref.at[pl.ds(i * R, R), pl.ds(at, width)],
                        sems.at[i, j],
                    )
                )
                at += width
        for copy in copies:
            copy.start()
        for copy in copies:
            copy.wait()

    in_hbm = pl.BlockSpec(memory_space=pltpu.HBM)
    return pl.pallas_call(
        kernel,
        out_shape=jax.ShapeDtypeStruct((per * R, total), jnp.bfloat16),
        in_specs=[pl.BlockSpec(memory_space=pltpu.SMEM)] + [in_hbm] * len(parts),
        out_specs=pl.BlockSpec(memory_space=pltpu.VMEM),
        scratch_shapes=[pltpu.SemaphoreType.DMA((per, len(parts)))],
        compiler_params=params(52),
        name="pick_rows",
    )(owners, *[store for store, _, _ in parts])


def rotate(matrix, basis, shard):
    rows = matrix.shape[0]
    blocks, width = basis.shape[0], basis.shape[1]
    each = max(n for n in range(1, 5) if blocks % n == 0 and n * width <= 1024)
    steps = blocks // each

    def kernel(shard_ref, matrix_ref, basis_ref, out_ref):
        for k in range(each):
            columns = slice(k * width, (k + 1) * width)
            turned = jnp.dot(
                matrix_ref[:, columns], basis_ref[k], preferred_element_type=jnp.float32
            )
            high = turned.astype(jnp.bfloat16)
            out_ref[:rows, columns] = high
            out_ref[rows:, columns] = (turned - high.astype(jnp.float32)).astype(jnp.bfloat16)

    total = blocks * width
    return pl.pallas_call(
        kernel,
        out_shape=jax.ShapeDtypeStruct((2 * rows, total), jnp.bfloat16),
        grid_spec=pltpu.PrefetchScalarGridSpec(
            num_scalar_prefetch=1,
            grid=(steps,),
            in_specs=[
                pl.BlockSpec((rows, each * width), lambda k, at: (0, at[0] * steps + k)),
                pl.BlockSpec((each, width, width), lambda k, at: (k, 0, 0)),
            ],
            out_specs=pl.BlockSpec((2 * rows, each * width), lambda k, at: (0, k)),
        ),
        compiler_params=params(56),
        cost_estimate=pl.CostEstimate(
            flops=2 * rows * total * width,
            bytes_accessed=2 * (3 * rows * total + total * width),
            transcendentals=0,
        ),
        name="rotate",
    )(jnp.reshape(shard, (1,)).astype(jnp.int32), matrix, basis)


def contract_rows(both, second):
    rows = both.shape[0] // 2
    out = lax.dot_general(
        both, second, (((1,), (1,)), ((), ())), preferred_element_type=jnp.float32
    )
    return out[:rows] + out[rows:]


def score(coefficients, projected, hit):
    sequences = coefficients[0].shape[0] // LEN
    count = len(coefficients)

    def kernel(hit_ref, *refs):
        out = jnp.zeros((sequences, NQ), jnp.float32)
        at = 0
        which, base = 0, 0
        for part_ref in refs[count:-1]:
            width = part_ref.shape[1]
            if base == refs[which].shape[1]:
                which, base = which + 1, 0
            terms = refs[which][:, base : base + width] * part_ref[...]
            base += width
            out += jnp.dot(
                jnp.sum(terms.reshape(sequences, LEN, width), axis=1) * (1.0 / LEN),
                hit_ref[at : at + width, :],
                precision=lax.Precision.HIGHEST,
                preferred_element_type=jnp.float32,
            )
            at += width
        refs[-1][...] = out

    return pl.pallas_call(
        kernel,
        out_shape=jax.ShapeDtypeStruct((sequences, NQ), jnp.float32),
        compiler_params=params(32),
        name="score",
    )(hit, *coefficients, *projected)


def places(owners):
    at = jnp.arange(NQ, dtype=jnp.int32)
    before = (owners[None, :] < owners[:, None]) | (
        (owners[None, :] == owners[:, None]) & (at[None, :] < at[:, None])
    )
    return jnp.sum(before.astype(jnp.int32), axis=1)


def swapped(piece, distance, shards):
    return lax.ppermute(piece, "mp", [(i, i ^ distance) for i in range(shards)])


def small_sum(array, shards, most, distance=1):
    while distance < shards:
        reach = min(most, shards // distance)
        array = sum([swapped(array, distance * k, shards) for k in range(1, reach)], array)
        distance *= reach
    return array


def after(value, others):
    return lax.optimization_barrier((value, others))[0] if jax.tree.leaves(others) else value


def sum_over_shards(matrix, shards):
    shard = lax.axis_index("mp")
    bit = shard % 2
    half = matrix.shape[0] // 2
    mine = lax.dynamic_slice_in_dim(matrix, bit * half, half, 0)
    mine = mine + swapped(lax.dynamic_slice_in_dim(matrix, (1 - bit) * half, half, 0), 1, shards)
    mine = small_sum(mine, shards, 2, 2)
    other = swapped(mine, 1, shards)
    return jnp.where(
        bit == 0, jnp.concatenate([mine, other], axis=0), jnp.concatenate([other, mine], axis=0)
    )


def on_device(groups, shards, out_grads, hidden_acts, out_basis, in_basis, left_store, right_store, owners):
    per = NQ // groups
    group = lax.axis_index("dp")
    shard = lax.axis_index("mp")
    place = places(owners)
    chunk = per * R
    ring = list(range(0, groups, 2)) + list(range(groups - 1, 0, -2))
    forward = [(ring[i], ring[(i + 1) % groups]) for i in range(groups)]
    backward = [(b, a) for a, b in forward]
    reach = groups // 2

    width_left = left_store.shape[2]
    width_right = right_store.shape[2]
    cut = max(width_right * 5 // 14 // 128 * 128, 128)
    own = [pick_rows(groups, owners, [(left_store, 0, width_left), (right_store, 0, cut)])]
    grads = rotate(out_grads, out_basis, shard)
    own.append(
        pick_rows(groups, after(owners, grads), [(right_store, cut, width_right - cut)])
    )

    steps = [[], []]
    came = []

    def send(piece, hops, others):
        ahead, behind = steps[piece][-1] if hops > 1 else (own[piece], own[piece])
        if hops == reach:
            ahead, behind = ahead[: chunk // 2], behind[chunk // 2 :]
        ahead, behind = after((ahead, behind), others)
        got = (lax.ppermute(ahead, "dp", forward), lax.ppermute(behind, "dp", backward))
        steps[piece].append(got)
        came.append(got)

    def side_by_side(step):
        return jnp.concatenate(step, axis=0)

    acts = rotate(hidden_acts, in_basis, 0)

    for hops in range(1, reach):
        send(0, hops, came[-3:-1])
        send(1, hops, came[-3:-1])
    own_later = after(own, came[0])
    first = [side_by_side(step) for step in steps[0][:-1]] + [own_later[0]]
    second = [side_by_side(step) for step in steps[1][:-1]] + [own_later[1]]
    left_fac = jnp.concatenate([part[:, :width_left] for part in first], axis=0)
    coefficients = [sum_over_shards(contract_rows(grads, left_fac), shards)]
    send(0, reach, came[-3:-1] + coefficients)

    first.append(side_by_side(steps[0][reach - 2]))
    part = contract_rows(grads, first[-1][:, :width_left])
    coefficients.append(small_sum(part, shards, 2))
    send(1, reach, came[-3:-1])

    last = after(steps[0][-1], came[-3])
    second.append(side_by_side(after(steps[1][reach - 2], last)))
    last = side_by_side(last)
    part = contract_rows(grads, last[:, :width_left])
    part = part + swapped(part, 1, shards)
    first.append(after(last, part))
    second.append(side_by_side(after(steps[1][-1], part)))
    coefficients.append(small_sum(part, shards, 2, 2))

    projected = [
        contract_rows(acts[:, :cut], one[:, width_left:]) + contract_rows(acts[:, cut:], other)
        for one, other in zip(first, second)
    ]

    def position(index):
        return jnp.where(index % 2 == 0, index // 2, groups - 1 - index // 2)

    here = position(group)
    row = jnp.arange(chunk, dtype=jnp.int32) // R
    sources = []
    for hops in range(1, reach):
        if hops == reach - 1:
            sources.append((here + 0 * row, row))
        sources += [(here - hops + 0 * row, row), (here + hops + 0 * row, row)]
    half = chunk // 2
    sources += [(here - reach + 0 * row[:half], row[:half]), (here + reach + 0 * row[half:], row[half:])]
    source = jnp.concatenate([s for s, _ in sources]) % groups
    row = jnp.concatenate([r for _, r in sources])
    owner = place // per
    hit = (source[:, None] == position(owner)[None, :]) & (row[:, None] == (place % per)[None, :])
    scores = score(coefficients, projected, hit.astype(jnp.float32))
    return small_sum(scores, shards, 4)


def solution(mesh):
    groups = mesh.shape["dp"]
    shards = mesh.shape["mp"]
    in_specs = (
        P("dp", None),
        P("dp", "mp"),
        P("mp", None, None),
        P("mp", None, None),
        P("dp", None, "mp"),
        P("dp", None, "mp"),
        P(),
    )

    def whole(*arrays):
        return on_device(groups, shards, *arrays)

    return jax.shard_map(
        whole, mesh=mesh, in_specs=in_specs, out_specs=P("dp", None), check_vma=False
    )
```

```python
import jax
import jax.numpy as jnp
from jax import lax
from jax.experimental import pallas as pl
from jax.experimental.pallas import tpu as pltpu
from jax.sharding import PartitionSpec as P

NQ = 16
R = 32
LEN = 128


def params(mebibytes):
    return pltpu.CompilerParams(vmem_limit_bytes=mebibytes * 2**20)


def pick_rows(groups, owners, parts):
    per = NQ // groups
    total = sum(width for _, _, width in parts)

    def kernel(owners_ref, *refs):
        stores, out_ref, sems = refs[:-2], refs[-2], refs[-1]
        group = lax.axis_index("dp")
        found = jnp.int32(0)
        queries = [jnp.int32(0)] * per
        for q in range(NQ):
            own = owners_ref[q] == group
            queries = [jnp.where(own & (found == i), q, at) for i, at in enumerate(queries)]
            found = found + own.astype(jnp.int32)
        copies = []
        for i in range(per):
            rows = pl.ds(pl.multiple_of(queries[i] * R, R), R)
            at = 0
            for j, (store_ref, (_, base, width)) in enumerate(zip(stores, parts)):
                copies.append(
                    pltpu.make_async_copy(
                        store_ref.at[0, rows, pl.ds(base, width)],
                        out_ref.at[pl.ds(i * R, R), pl.ds(at, width)],
                        sems.at[i, j],
                    )
                )
                at += width
        for copy in copies:
            copy.start()
        for copy in copies:
            copy.wait()

    in_hbm = pl.BlockSpec(memory_space=pltpu.HBM)
    return pl.pallas_call(
        kernel,
        out_shape=jax.ShapeDtypeStruct((per * R, total), jnp.bfloat16),
        in_specs=[pl.BlockSpec(memory_space=pltpu.SMEM)] + [in_hbm] * len(parts),
        out_specs=pl.BlockSpec(memory_space=pltpu.VMEM),
        scratch_shapes=[pltpu.SemaphoreType.DMA((per, len(parts)))],
        compiler_params=params(52),
        name="pick_rows",
    )(owners, *[store for store, _, _ in parts])


def rotate(matrix, basis, shard):
    rows = matrix.shape[0]
    blocks, width = basis.shape[0], basis.shape[1]
    each = max(n for n in range(1, 5) if blocks % n == 0 and n * width <= 1024)
    steps = blocks // each

    def kernel(shard_ref, matrix_ref, basis_ref, out_ref):
        for k in range(each):
            columns = slice(k * width, (k + 1) * width)
            turned = jnp.dot(
                matrix_ref[:, columns], basis_ref[k], preferred_element_type=jnp.float32
            )
            high = turned.astype(jnp.bfloat16)
            out_ref[:rows, columns] = high
            out_ref[rows:, columns] = (turned - high.astype(jnp.float32)).astype(jnp.bfloat16)

    total = blocks * width
    return pl.pallas_call(
        kernel,
        out_shape=jax.ShapeDtypeStruct((2 * rows, total), jnp.bfloat16),
        grid_spec=pltpu.PrefetchScalarGridSpec(
            num_scalar_prefetch=1,
            grid=(steps,),
            in_specs=[
                pl.BlockSpec((rows, each * width), lambda k, at: (0, at[0] * steps + k)),
                pl.BlockSpec((each, width, width), lambda k, at: (k, 0, 0)),
            ],
            out_specs=pl.BlockSpec((2 * rows, each * width), lambda k, at: (0, k)),
        ),
        compiler_params=params(56),
        cost_estimate=pl.CostEstimate(
            flops=2 * rows * total * width,
            bytes_accessed=2 * (3 * rows * total + total * width),
            transcendentals=0,
        ),
        name="rotate",
    )(jnp.reshape(shard, (1,)).astype(jnp.int32), matrix, basis)


def contract_rows(both, second):
    rows = both.shape[0] // 2
    out = lax.dot_general(
        both, second, (((1,), (1,)), ((), ())), preferred_element_type=jnp.float32
    )
    return out[:rows] + out[rows:]


def score(coefficients, projected, hit):
    sequences = coefficients[0].shape[0] // LEN
    count = len(coefficients)

    def kernel(hit_ref, *refs):
        out = jnp.zeros((sequences, NQ), jnp.float32)
        at = 0
        which, base = 0, 0
        for part_ref in refs[count:-1]:
            width = part_ref.shape[1]
            if base == refs[which].shape[1]:
                which, base = which + 1, 0
            terms = refs[which][:, base : base + width] * part_ref[...]
            base += width
            out += jnp.dot(
                jnp.sum(terms.reshape(sequences, LEN, width), axis=1) * (1.0 / LEN),
                hit_ref[at : at + width, :],
                precision=lax.Precision.HIGHEST,
                preferred_element_type=jnp.float32,
            )
            at += width
        refs[-1][...] = out

    return pl.pallas_call(
        kernel,
        out_shape=jax.ShapeDtypeStruct((sequences, NQ), jnp.float32),
        compiler_params=params(32),
        name="score",
    )(hit, *coefficients, *projected)


def places(owners):
    at = jnp.arange(NQ, dtype=jnp.int32)
    before = (owners[None, :] < owners[:, None]) | (
        (owners[None, :] == owners[:, None]) & (at[None, :] < at[:, None])
    )
    return jnp.sum(before.astype(jnp.int32), axis=1)


def swapped(piece, distance, shards):
    return lax.ppermute(piece, "mp", [(i, i ^ distance) for i in range(shards)])


def small_sum(array, shards, most, distance=1):
    while distance < shards:
        reach = min(most, shards // distance)
        array = sum([swapped(array, distance * k, shards) for k in range(1, reach)], array)
        distance *= reach
    return array


def after(value, others):
    return lax.optimization_barrier((value, others))[0] if jax.tree.leaves(others) else value


def sum_over_shards(matrix, shards):
    shard = lax.axis_index("mp")
    bit = shard % 2
    half = matrix.shape[0] // 2
    mine = lax.dynamic_slice_in_dim(matrix, bit * half, half, 0)
    mine = mine + swapped(lax.dynamic_slice_in_dim(matrix, (1 - bit) * half, half, 0), 1, shards)
    mine = small_sum(mine, shards, 2, 2)
    other = swapped(mine, 1, shards)
    return jnp.where(
        bit == 0, jnp.concatenate([mine, other], axis=0), jnp.concatenate([other, mine], axis=0)
    )


def on_device(groups, shards, out_grads, hidden_acts, out_basis, in_basis, left_store, right_store, owners):
    per = NQ // groups
    group = lax.axis_index("dp")
    shard = lax.axis_index("mp")
    place = places(owners)
    chunk = per * R
    ring = list(range(0, groups, 2)) + list(range(groups - 1, 0, -2))
    forward = [(ring[i], ring[(i + 1) % groups]) for i in range(groups)]
    backward = [(b, a) for a, b in forward]
    reach = groups // 2

    width_left = left_store.shape[2]
    width_right = right_store.shape[2]
    cut = max(width_right * 5 // 14 // 128 * 128, 128)
    own = [pick_rows(groups, owners, [(left_store, 0, width_left), (right_store, 0, cut)])]
    grads = rotate(out_grads, out_basis, shard)
    own.append(
        pick_rows(groups, after(owners, grads), [(right_store, cut, width_right - cut)])
    )

    steps = [[], []]
    came = []

    def send(piece, hops, others):
        ahead, behind = steps[piece][-1] if hops > 1 else (own[piece], own[piece])
        if hops == reach:
            ahead, behind = ahead[: chunk // 2], behind[chunk // 2 :]
        ahead, behind = after((ahead, behind), others)
        got = (lax.ppermute(ahead, "dp", forward), lax.ppermute(behind, "dp", backward))
        steps[piece].append(got)
        came.append(got)

    def side_by_side(step):
        return jnp.concatenate(step, axis=0)

    acts = rotate(hidden_acts, in_basis, 0)

    for hops in range(1, reach):
        send(0, hops, came[-3:-1])
        send(1, hops, came[-3:-1])
    own_later = after(own, came[0])
    first = [side_by_side(step) for step in steps[0][:-1]] + [own_later[0]]
    second = [side_by_side(step) for step in steps[1][:-1]] + [own_later[1]]
    left_fac = jnp.concatenate([part[:, :width_left] for part in first], axis=0)
    coefficients = [sum_over_shards(contract_rows(grads, left_fac), shards)]
    send(0, reach, came[-3:-1] + coefficients)

    first.append(side_by_side(steps[0][reach - 2]))
    part = contract_rows(grads, first[-1][:, :width_left])
    coefficients.append(small_sum(part, shards, 2))
    send(1, reach, came[-3:-1])

    last = after(steps[0][-1], came[-3])
    second.append(side_by_side(after(steps[1][reach - 2], last)))
    last = side_by_side(last)
    part = contract_rows(grads, last[:, :width_left])
    last_sum = small_sum(part, shards, 4)
    first.append(after(last, part))
    second.append(side_by_side(steps[1][-1]))
    coefficients.append(last_sum)

    projected = [
        contract_rows(acts[:, :cut], one[:, width_left:]) + contract_rows(acts[:, cut:], other)
        for one, other in zip(first, second)
    ]

    def position(index):
        return jnp.where(index % 2 == 0, index // 2, groups - 1 - index // 2)

    here = position(group)
    row = jnp.arange(chunk, dtype=jnp.int32) // R
    sources = []
    for hops in range(1, reach):
        if hops == reach - 1:
            sources.append((here + 0 * row, row))
        sources += [(here - hops + 0 * row, row), (here + hops + 0 * row, row)]
    half = chunk // 2
    sources += [(here - reach + 0 * row[:half], row[:half]), (here + reach + 0 * row[half:], row[half:])]
    source = jnp.concatenate([s for s, _ in sources]) % groups
    row = jnp.concatenate([r for _, r in sources])
    owner = place // per
    hit = (source[:, None] == position(owner)[None, :]) & (row[:, None] == (place % per)[None, :])
    scores = score(coefficients, projected, hit.astype(jnp.float32))
    return small_sum(scores, shards, 4)


def solution(mesh):
    groups = mesh.shape["dp"]
    shards = mesh.shape["mp"]
    in_specs = (
        P("dp", None),
        P("dp", "mp"),
        P("mp", None, None),
        P("mp", None, None),
        P("dp", None, "mp"),
        P("dp", None, "mp"),
        P(),
    )

    def whole(*arrays):
        return on_device(groups, shards, *arrays)

    return jax.shard_map(
        whole, mesh=mesh, in_specs=in_specs, out_specs=P("dp", None), check_vma=False
    )
```

```python
import jax
import jax.numpy as jnp
from jax import lax
from jax.experimental import pallas as pl
from jax.experimental.pallas import tpu as pltpu
from jax.sharding import PartitionSpec as P

NQ = 16
R = 32
LEN = 128


def params(mebibytes):
    return pltpu.CompilerParams(vmem_limit_bytes=mebibytes * 2**20)


def pick_rows(groups, owners, parts):
    per = NQ // groups
    total = sum(width for _, _, width in parts)

    def kernel(owners_ref, *refs):
        stores, out_ref, sems = refs[:-2], refs[-2], refs[-1]
        group = lax.axis_index("dp")
        found = jnp.int32(0)
        queries = [jnp.int32(0)] * per
        for q in range(NQ):
            own = owners_ref[q] == group
            queries = [jnp.where(own & (found == i), q, at) for i, at in enumerate(queries)]
            found = found + own.astype(jnp.int32)
        copies = []
        for i in range(per):
            rows = pl.ds(pl.multiple_of(queries[i] * R, R), R)
            at = 0
            for j, (store_ref, (_, base, width)) in enumerate(zip(stores, parts)):
                copies.append(
                    pltpu.make_async_copy(
                        store_ref.at[0, rows, pl.ds(base, width)],
                        out_ref.at[pl.ds(i * R, R), pl.ds(at, width)],
                        sems.at[i, j],
                    )
                )
                at += width
        for copy in copies:
            copy.start()
        for copy in copies:
            copy.wait()

    in_hbm = pl.BlockSpec(memory_space=pltpu.HBM)
    return pl.pallas_call(
        kernel,
        out_shape=jax.ShapeDtypeStruct((per * R, total), jnp.bfloat16),
        in_specs=[pl.BlockSpec(memory_space=pltpu.SMEM)] + [in_hbm] * len(parts),
        out_specs=pl.BlockSpec(memory_space=pltpu.VMEM),
        scratch_shapes=[pltpu.SemaphoreType.DMA((per, len(parts)))],
        compiler_params=params(52),
        name="pick_rows",
    )(owners, *[store for store, _, _ in parts])


def rotate(matrix, basis, shard):
    rows = matrix.shape[0]
    blocks, width = basis.shape[0], basis.shape[1]
    each = max(n for n in range(1, 5) if blocks % n == 0 and n * width <= 1024)
    steps = blocks // each

    def kernel(shard_ref, matrix_ref, basis_ref, out_ref):
        for k in range(each):
            columns = slice(k * width, (k + 1) * width)
            turned = jnp.dot(
                matrix_ref[:, columns], basis_ref[k], preferred_element_type=jnp.float32
            )
            high = turned.astype(jnp.bfloat16)
            out_ref[:rows, columns] = high
            out_ref[rows:, columns] = (turned - high.astype(jnp.float32)).astype(jnp.bfloat16)

    total = blocks * width
    return pl.pallas_call(
        kernel,
        out_shape=jax.ShapeDtypeStruct((2 * rows, total), jnp.bfloat16),
        grid_spec=pltpu.PrefetchScalarGridSpec(
            num_scalar_prefetch=1,
            grid=(steps,),
            in_specs=[
                pl.BlockSpec((rows, each * width), lambda k, at: (0, at[0] * steps + k)),
                pl.BlockSpec((each, width, width), lambda k, at: (k, 0, 0)),
            ],
            out_specs=pl.BlockSpec((2 * rows, each * width), lambda k, at: (0, k)),
        ),
        compiler_params=params(56),
        cost_estimate=pl.CostEstimate(
            flops=2 * rows * total * width,
            bytes_accessed=2 * (3 * rows * total + total * width),
            transcendentals=0,
        ),
        name="rotate",
    )(jnp.reshape(shard, (1,)).astype(jnp.int32), matrix, basis)


def contract_rows(both, second):
    rows = both.shape[0] // 2
    out = lax.dot_general(
        both, second, (((1,), (1,)), ((), ())), preferred_element_type=jnp.float32
    )
    return out[:rows] + out[rows:]


def score(coefficients, projected, hit):
    sequences = projected[0].shape[0] // LEN
    count = len(coefficients)

    def kernel(hit_ref, *refs):
        out = jnp.zeros((sequences, NQ), jnp.float32)
        at = 0
        which, base = 0, 0
        for part_ref in refs[count:-1]:
            width = part_ref.shape[1]
            if base == refs[which].shape[1]:
                which, base = which + 1, 0
            if which < count - 1:
                terms = (refs[which][:, base : base + width] * part_ref[...]).reshape(sequences, LEN, width)
                base += width
            else:
                terms = jnp.stack(
                    [
                        refs[which][:, i * width : (i + 1) * width] * part_ref[i * LEN : (i + 1) * LEN, :]
                        for i in range(sequences)
                    ]
                )
            out += jnp.dot(
                jnp.sum(terms, axis=1) * (1.0 / LEN),
                hit_ref[at : at + width, :],
                precision=lax.Precision.HIGHEST,
                preferred_element_type=jnp.float32,
            )
            at += width
        refs[-1][...] = out

    return pl.pallas_call(
        kernel,
        out_shape=jax.ShapeDtypeStruct((sequences, NQ), jnp.float32),
        compiler_params=params(32),
        name="score",
    )(hit, *coefficients, *projected)


def places(owners):
    at = jnp.arange(NQ, dtype=jnp.int32)
    before = (owners[None, :] < owners[:, None]) | (
        (owners[None, :] == owners[:, None]) & (at[None, :] < at[:, None])
    )
    return jnp.sum(before.astype(jnp.int32), axis=1)


def swapped(piece, distance, shards):
    return lax.ppermute(piece, "mp", [(i, i ^ distance) for i in range(shards)])


def small_sum(array, shards, most, distance=1):
    while distance < shards:
        reach = min(most, shards // distance)
        array = sum([swapped(array, distance * k, shards) for k in range(1, reach)], array)
        distance *= reach
    return array


def after(value, others):
    return lax.optimization_barrier((value, others))[0] if jax.tree.leaves(others) else value


def sum_over_shards(matrix, shards):
    shard = lax.axis_index("mp")
    bit = shard % 2
    half = matrix.shape[0] // 2
    mine = lax.dynamic_slice_in_dim(matrix, bit * half, half, 0)
    mine = mine + swapped(lax.dynamic_slice_in_dim(matrix, (1 - bit) * half, half, 0), 1, shards)
    mine = small_sum(mine, shards, 2, 2)
    other = swapped(mine, 1, shards)
    return jnp.where(
        bit == 0, jnp.concatenate([mine, other], axis=0), jnp.concatenate([other, mine], axis=0)
    )


def on_device(groups, shards, out_grads, hidden_acts, out_basis, in_basis, left_store, right_store, owners):
    per = NQ // groups
    group = lax.axis_index("dp")
    shard = lax.axis_index("mp")
    place = places(owners)
    chunk = per * R
    ring = list(range(0, groups, 2)) + list(range(groups - 1, 0, -2))
    forward = [(ring[i], ring[(i + 1) % groups]) for i in range(groups)]
    backward = [(b, a) for a, b in forward]
    reach = groups // 2

    width_left = left_store.shape[2]
    width_right = right_store.shape[2]
    cut = max(width_right * 5 // 14 // 128 * 128, 128)
    own = [pick_rows(groups, owners, [(left_store, 0, width_left), (right_store, 0, cut)])]
    grads = rotate(out_grads, out_basis, shard)
    own.append(
        pick_rows(groups, after(owners, grads), [(right_store, cut, width_right - cut)])
    )

    steps = [[], []]
    came = []

    def send(piece, hops, others):
        ahead, behind = steps[piece][-1] if hops > 1 else (own[piece], own[piece])
        if hops == reach:
            ahead, behind = ahead[: chunk // 2], behind[chunk // 2 :]
        ahead, behind = after((ahead, behind), others)
        got = (lax.ppermute(ahead, "dp", forward), lax.ppermute(behind, "dp", backward))
        steps[piece].append(got)
        came.append(got)

    def side_by_side(step):
        return jnp.concatenate(step, axis=0)

    acts = rotate(hidden_acts, in_basis, 0)

    for hops in range(1, reach):
        send(0, hops, came[-3:-1])
        send(1, hops, came[-3:-1])
    own_later = after(own, came[0])
    first = [side_by_side(step) for step in steps[0][:-1]] + [own_later[0]]
    second = [side_by_side(step) for step in steps[1][:-1]] + [own_later[1]]
    left_fac = jnp.concatenate([part[:, :width_left] for part in first], axis=0)
    coefficients = [sum_over_shards(contract_rows(grads, left_fac), shards)]
    send(0, reach, came[-3:-1] + coefficients)

    first.append(side_by_side(steps[0][reach - 2]))
    part = contract_rows(grads, first[-1][:, :width_left])
    coefficients.append(small_sum(part, shards, 2))
    send(1, reach, came[-3:-1])

    last = after(steps[0][-1], came[-3])
    second.append(side_by_side(after(steps[1][reach - 2], last)))
    last = side_by_side(last)
    part = contract_rows(grads, last[:, :width_left]).reshape(-1, LEN, chunk)
    part = jnp.concatenate([part[i] for i in range(part.shape[0])], axis=1)
    last_sum = small_sum(part, shards, 4)
    first.append(after(last, part))
    second.append(side_by_side(steps[1][-1]))
    coefficients.append(last_sum)

    projected = [
        contract_rows(acts[:, :cut], one[:, width_left:]) + contract_rows(acts[:, cut:], other)
        for one, other in zip(first, second)
    ]

    def position(index):
        return jnp.where(index % 2 == 0, index // 2, groups - 1 - index // 2)

    here = position(group)
    row = jnp.arange(chunk, dtype=jnp.int32) // R
    sources = []
    for hops in range(1, reach):
        if hops == reach - 1:
            sources.append((here + 0 * row, row))
        sources += [(here - hops + 0 * row, row), (here + hops + 0 * row, row)]
    half = chunk // 2
    sources += [(here - reach + 0 * row[:half], row[:half]), (here + reach + 0 * row[half:], row[half:])]
    source = jnp.concatenate([s for s, _ in sources]) % groups
    row = jnp.concatenate([r for _, r in sources])
    owner = place // per
    hit = (source[:, None] == position(owner)[None, :]) & (row[:, None] == (place % per)[None, :])
    scores = score(coefficients, projected, hit.astype(jnp.float32))
    return small_sum(scores, shards, 4)


def solution(mesh):
    groups = mesh.shape["dp"]
    shards = mesh.shape["mp"]
    in_specs = (
        P("dp", None),
        P("dp", "mp"),
        P("mp", None, None),
        P("mp", None, None),
        P("dp", None, "mp"),
        P("dp", None, "mp"),
        P(),
    )

    def whole(*arrays):
        return on_device(groups, shards, *arrays)

    return jax.shard_map(
        whole, mesh=mesh, in_specs=in_specs, out_specs=P("dp", None), check_vma=False
    )
```

```python
import jax
import jax.numpy as jnp
from jax import lax
from jax.experimental import pallas as pl
from jax.experimental.pallas import tpu as pltpu
from jax.sharding import PartitionSpec as P

NQ = 16
R = 32
LEN = 128


def params(mebibytes):
    return pltpu.CompilerParams(vmem_limit_bytes=mebibytes * 2**20)


def pick_rows(groups, owners, parts):
    per = NQ // groups
    total = sum(width for _, _, width in parts)

    def kernel(owners_ref, *refs):
        stores, out_ref, sems = refs[:-2], refs[-2], refs[-1]
        group = lax.axis_index("dp")
        found = jnp.int32(0)
        queries = [jnp.int32(0)] * per
        for q in range(NQ):
            own = owners_ref[q] == group
            queries = [jnp.where(own & (found == i), q, at) for i, at in enumerate(queries)]
            found = found + own.astype(jnp.int32)
        copies = []
        for i in range(per):
            rows = pl.ds(pl.multiple_of(queries[i] * R, R), R)
            at = 0
            for j, (store_ref, (_, base, width)) in enumerate(zip(stores, parts)):
                copies.append(
                    pltpu.make_async_copy(
                        store_ref.at[0, rows, pl.ds(base, width)],
                        out_ref.at[pl.ds(i * R, R), pl.ds(at, width)],
                        sems.at[i, j],
                    )
                )
                at += width
        for copy in copies:
            copy.start()
        for copy in copies:
            copy.wait()

    in_hbm = pl.BlockSpec(memory_space=pltpu.HBM)
    return pl.pallas_call(
        kernel,
        out_shape=jax.ShapeDtypeStruct((per * R, total), jnp.bfloat16),
        in_specs=[pl.BlockSpec(memory_space=pltpu.SMEM)] + [in_hbm] * len(parts),
        out_specs=pl.BlockSpec(memory_space=pltpu.VMEM),
        scratch_shapes=[pltpu.SemaphoreType.DMA((per, len(parts)))],
        compiler_params=params(52),
        name="pick_rows",
    )(owners, *[store for store, _, _ in parts])


def rotate(matrix, basis, shard):
    rows = matrix.shape[0]
    blocks, width = basis.shape[0], basis.shape[1]
    each = max(n for n in range(1, 5) if blocks % n == 0 and n * width <= 1024)
    steps = blocks // each

    def kernel(shard_ref, matrix_ref, basis_ref, out_ref):
        for k in range(each):
            columns = slice(k * width, (k + 1) * width)
            turned = jnp.dot(
                matrix_ref[:, columns], basis_ref[k], preferred_element_type=jnp.float32
            )
            high = turned.astype(jnp.bfloat16)
            out_ref[:rows, columns] = high
            out_ref[rows:, columns] = (turned - high.astype(jnp.float32)).astype(jnp.bfloat16)

    total = blocks * width
    return pl.pallas_call(
        kernel,
        out_shape=jax.ShapeDtypeStruct((2 * rows, total), jnp.bfloat16),
        grid_spec=pltpu.PrefetchScalarGridSpec(
            num_scalar_prefetch=1,
            grid=(steps,),
            in_specs=[
                pl.BlockSpec((rows, each * width), lambda k, at: (0, at[0] * steps + k)),
                pl.BlockSpec((each, width, width), lambda k, at: (k, 0, 0)),
            ],
            out_specs=pl.BlockSpec((2 * rows, each * width), lambda k, at: (0, k)),
        ),
        compiler_params=params(56),
        cost_estimate=pl.CostEstimate(
            flops=2 * rows * total * width,
            bytes_accessed=2 * (3 * rows * total + total * width),
            transcendentals=0,
        ),
        name="rotate",
    )(jnp.reshape(shard, (1,)).astype(jnp.int32), matrix, basis)


def contract_rows(both, second):
    rows = both.shape[0] // 2
    out = lax.dot_general(
        both, second, (((1,), (1,)), ((), ())), preferred_element_type=jnp.float32
    )
    return out[:rows] + out[rows:]


def score(coefficients, projected, hit):
    sequences = projected[0].shape[0] // LEN
    count = len(coefficients)

    def kernel(hit_ref, *refs):
        out = jnp.zeros((sequences, NQ), jnp.float32)
        at = 0
        which, base = 0, 0
        for part_ref in refs[count:-1]:
            width = part_ref.shape[1]
            if base == refs[which].shape[1]:
                which, base = which + 1, 0
            if which < count - 1:
                terms = (refs[which][:, base : base + width] * part_ref[...]).reshape(sequences, LEN, width)
                base += width
            else:
                terms = jnp.stack(
                    [
                        refs[which][:, i * width : (i + 1) * width] * part_ref[i * LEN : (i + 1) * LEN, :]
                        for i in range(sequences)
                    ]
                )
            out += jnp.dot(
                jnp.sum(terms, axis=1) * (1.0 / LEN),
                hit_ref[at : at + width, :],
                precision=lax.Precision.HIGHEST,
                preferred_element_type=jnp.float32,
            )
            at += width
        refs[-1][...] = out

    return pl.pallas_call(
        kernel,
        out_shape=jax.ShapeDtypeStruct((sequences, NQ), jnp.float32),
        compiler_params=params(32),
        name="score",
    )(hit, *coefficients, *projected)


def places(owners):
    at = jnp.arange(NQ, dtype=jnp.int32)
    before = (owners[None, :] < owners[:, None]) | (
        (owners[None, :] == owners[:, None]) & (at[None, :] < at[:, None])
    )
    return jnp.sum(before.astype(jnp.int32), axis=1)


def swapped(piece, distance, shards):
    return lax.ppermute(piece, "mp", [(i, i ^ distance) for i in range(shards)])


def small_sum(array, shards, most, distance=1):
    while distance < shards:
        reach = min(most, shards // distance)
        array = sum([swapped(array, distance * k, shards) for k in range(1, reach)], array)
        distance *= reach
    return array


def after(value, others):
    return lax.optimization_barrier((value, others))[0] if jax.tree.leaves(others) else value


def sum_over_shards(matrix, shards):
    shard = lax.axis_index("mp")
    bit = shard % 2
    half = matrix.shape[0] // 2
    mine = lax.dynamic_slice_in_dim(matrix, bit * half, half, 0)
    mine = mine + swapped(lax.dynamic_slice_in_dim(matrix, (1 - bit) * half, half, 0), 1, shards)
    mine = small_sum(mine, shards, 2, 2)
    other = swapped(mine, 1, shards)
    return jnp.where(
        bit == 0, jnp.concatenate([mine, other], axis=0), jnp.concatenate([other, mine], axis=0)
    )


def on_device(groups, shards, out_grads, hidden_acts, out_basis, in_basis, left_store, right_store, owners):
    per = NQ // groups
    group = lax.axis_index("dp")
    shard = lax.axis_index("mp")
    place = places(owners)
    chunk = per * R
    ring = list(range(0, groups, 2)) + list(range(groups - 1, 0, -2))
    forward = [(ring[i], ring[(i + 1) % groups]) for i in range(groups)]
    backward = [(b, a) for a, b in forward]
    reach = groups // 2

    width_left = left_store.shape[2]
    width_right = right_store.shape[2]
    cut = max(width_right * 5 // 14 // 128 * 128, 128)
    own = [pick_rows(groups, owners, [(left_store, 0, width_left), (right_store, 0, cut)])]
    grads = rotate(out_grads, out_basis, shard)
    own.append(
        pick_rows(groups, after(owners, grads), [(right_store, cut, width_right - cut)])
    )

    steps = [[], []]
    came = []

    def send(piece, hops, others):
        ahead, behind = steps[piece][-1] if hops > 1 else (own[piece], own[piece])
        if hops == reach:
            ahead, behind = ahead[: chunk // 2], behind[chunk // 2 :]
        ahead, behind = after((ahead, behind), others)
        got = (lax.ppermute(ahead, "dp", forward), lax.ppermute(behind, "dp", backward))
        steps[piece].append(got)
        came.append(got)

    def side_by_side(step):
        return jnp.concatenate(step, axis=0)

    acts = rotate(hidden_acts, in_basis, 0)

    for hops in range(1, reach):
        send(0, hops, came[-3:-1])
        send(1, hops, came[-3:-1])
    own_later = after(own, came[0])
    first = [side_by_side(step) for step in steps[0][:-1]] + [own_later[0]]
    second = [side_by_side(step) for step in steps[1][:-1]] + [own_later[1]]
    left_fac = jnp.concatenate([part[:, :width_left] for part in first], axis=0)
    coefficients = [sum_over_shards(contract_rows(grads, left_fac), shards)]
    send(0, reach, came[-3:-1] + coefficients)

    first.append(side_by_side(steps[0][reach - 2]))
    part = contract_rows(grads, first[-1][:, :width_left])
    coefficients.append(small_sum(part, shards, 2))
    send(1, reach, came[-3:-1])

    last = after(steps[0][-1], came[-3])
    second.append(side_by_side(after(steps[1][reach - 2], coefficients[1:2])))
    last = side_by_side(last)
    part = contract_rows(grads, last[:, :width_left]).reshape(-1, LEN, chunk)
    part = jnp.concatenate([part[i] for i in range(part.shape[0])], axis=1)
    last_sum = small_sum(part, shards, 4)
    first.append(after(last, part))
    second.append(side_by_side(steps[1][-1]))
    coefficients.append(last_sum)

    projected = [
        contract_rows(acts[:, :cut], one[:, width_left:]) + contract_rows(acts[:, cut:], other)
        for one, other in zip(first, second)
    ]

    def position(index):
        return jnp.where(index % 2 == 0, index // 2, groups - 1 - index // 2)

    here = position(group)
    row = jnp.arange(chunk, dtype=jnp.int32) // R
    sources = []
    for hops in range(1, reach):
        if hops == reach - 1:
            sources.append((here + 0 * row, row))
        sources += [(here - hops + 0 * row, row), (here + hops + 0 * row, row)]
    half = chunk // 2
    sources += [(here - reach + 0 * row[:half], row[:half]), (here + reach + 0 * row[half:], row[half:])]
    source = jnp.concatenate([s for s, _ in sources]) % groups
    row = jnp.concatenate([r for _, r in sources])
    owner = place // per
    hit = (source[:, None] == position(owner)[None, :]) & (row[:, None] == (place % per)[None, :])
    scores = score(coefficients, projected, hit.astype(jnp.float32))
    return small_sum(scores, shards, 4)


def solution(mesh):
    groups = mesh.shape["dp"]
    shards = mesh.shape["mp"]
    in_specs = (
        P("dp", None),
        P("dp", "mp"),
        P("mp", None, None),
        P("mp", None, None),
        P("dp", None, "mp"),
        P("dp", None, "mp"),
        P(),
    )

    def whole(*arrays):
        return on_device(groups, shards, *arrays)

    return jax.shard_map(
        whole, mesh=mesh, in_specs=in_specs, out_specs=P("dp", None), check_vma=False
    )
```

```python
import jax
import jax.numpy as jnp
from jax import lax
from jax.experimental import pallas as pl
from jax.experimental.pallas import tpu as pltpu
from jax.sharding import PartitionSpec as P

NQ = 16
R = 32
LEN = 128


def params(mebibytes):
    return pltpu.CompilerParams(vmem_limit_bytes=mebibytes * 2**20)


def pick_rows(groups, owners, parts):
    per = NQ // groups
    total = sum(width for _, _, width in parts)

    def kernel(owners_ref, *refs):
        stores, out_ref, sems = refs[:-2], refs[-2], refs[-1]
        group = lax.axis_index("dp")
        found = jnp.int32(0)
        queries = [jnp.int32(0)] * per
        for q in range(NQ):
            own = owners_ref[q] == group
            queries = [jnp.where(own & (found == i), q, at) for i, at in enumerate(queries)]
            found = found + own.astype(jnp.int32)
        copies = []
        for i in range(per):
            rows = pl.ds(pl.multiple_of(queries[i] * R, R), R)
            at = 0
            for j, (store_ref, (_, base, width)) in enumerate(zip(stores, parts)):
                copies.append(
                    pltpu.make_async_copy(
                        store_ref.at[0, rows, pl.ds(base, width)],
                        out_ref.at[pl.ds(i * R, R), pl.ds(at, width)],
                        sems.at[i, j],
                    )
                )
                at += width
        for copy in copies:
            copy.start()
        for copy in copies:
            copy.wait()

    in_hbm = pl.BlockSpec(memory_space=pltpu.HBM)
    return pl.pallas_call(
        kernel,
        out_shape=jax.ShapeDtypeStruct((per * R, total), jnp.bfloat16),
        in_specs=[pl.BlockSpec(memory_space=pltpu.SMEM)] + [in_hbm] * len(parts),
        out_specs=pl.BlockSpec(memory_space=pltpu.VMEM),
        scratch_shapes=[pltpu.SemaphoreType.DMA((per, len(parts)))],
        compiler_params=params(52),
        name="pick_rows",
    )(owners, *[store for store, _, _ in parts])


def rotate(matrix, basis, shard):
    rows = matrix.shape[0]
    blocks, width = basis.shape[0], basis.shape[1]
    each = max(n for n in range(1, 5) if blocks % n == 0 and n * width <= 1024)
    steps = blocks // each

    def kernel(shard_ref, matrix_ref, basis_ref, out_ref):
        for k in range(each):
            columns = slice(k * width, (k + 1) * width)
            turned = jnp.dot(
                matrix_ref[:, columns], basis_ref[k], preferred_element_type=jnp.float32
            )
            high = turned.astype(jnp.bfloat16)
            out_ref[:rows, columns] = high
            out_ref[rows:, columns] = (turned - high.astype(jnp.float32)).astype(jnp.bfloat16)

    total = blocks * width
    return pl.pallas_call(
        kernel,
        out_shape=jax.ShapeDtypeStruct((2 * rows, total), jnp.bfloat16),
        grid_spec=pltpu.PrefetchScalarGridSpec(
            num_scalar_prefetch=1,
            grid=(steps,),
            in_specs=[
                pl.BlockSpec((rows, each * width), lambda k, at: (0, at[0] * steps + k)),
                pl.BlockSpec((each, width, width), lambda k, at: (k, 0, 0)),
            ],
            out_specs=pl.BlockSpec((2 * rows, each * width), lambda k, at: (0, k)),
        ),
        compiler_params=params(56),
        cost_estimate=pl.CostEstimate(
            flops=2 * rows * total * width,
            bytes_accessed=2 * (3 * rows * total + total * width),
            transcendentals=0,
        ),
        name="rotate",
    )(jnp.reshape(shard, (1,)).astype(jnp.int32), matrix, basis)


def contract_rows(both, second):
    rows = both.shape[0] // 2
    out = lax.dot_general(
        both, second, (((1,), (1,)), ((), ())), preferred_element_type=jnp.float32
    )
    return out[:rows] + out[rows:]


def score(coefficients, projected, hit):
    sequences = projected[0].shape[0] // LEN
    count = len(coefficients)

    def kernel(hit_ref, *refs):
        out = jnp.zeros((sequences, NQ), jnp.float32)
        at = 0
        which, base = 0, 0
        for part_ref in refs[count:-1]:
            width = part_ref.shape[1]
            if base == refs[which].shape[1]:
                which, base = which + 1, 0
            if which < count - 1:
                terms = (refs[which][:, base : base + width] * part_ref[...]).reshape(sequences, LEN, width)
                base += width
            else:
                terms = jnp.stack(
                    [
                        refs[which][:, i * width : (i + 1) * width] * part_ref[i * LEN : (i + 1) * LEN, :]
                        for i in range(sequences)
                    ]
                )
            out += jnp.dot(
                jnp.sum(terms, axis=1) * (1.0 / LEN),
                hit_ref[at : at + width, :],
                precision=lax.Precision.HIGHEST,
                preferred_element_type=jnp.float32,
            )
            at += width
        refs[-1][...] = out

    return pl.pallas_call(
        kernel,
        out_shape=jax.ShapeDtypeStruct((sequences, NQ), jnp.float32),
        compiler_params=params(32),
        name="score",
    )(hit, *coefficients, *projected)


def places(owners):
    at = jnp.arange(NQ, dtype=jnp.int32)
    before = (owners[None, :] < owners[:, None]) | (
        (owners[None, :] == owners[:, None]) & (at[None, :] < at[:, None])
    )
    return jnp.sum(before.astype(jnp.int32), axis=1)


def swapped(piece, distance, shards):
    return lax.ppermute(piece, "mp", [(i, i ^ distance) for i in range(shards)])


def small_sum(array, shards, most, distance=1):
    while distance < shards:
        reach = min(most, shards // distance)
        array = sum([swapped(array, distance * k, shards) for k in range(1, reach)], array)
        distance *= reach
    return array


def after(value, others):
    return lax.optimization_barrier((value, others))[0] if jax.tree.leaves(others) else value


def sum_over_shards(matrix, shards):
    shard = lax.axis_index("mp")
    bit = shard % 2
    half = matrix.shape[0] // 2
    mine = lax.dynamic_slice_in_dim(matrix, bit * half, half, 0)
    mine = mine + swapped(lax.dynamic_slice_in_dim(matrix, (1 - bit) * half, half, 0), 1, shards)
    mine = small_sum(mine, shards, 2, 2)
    other = swapped(mine, 1, shards)
    return jnp.where(
        bit == 0, jnp.concatenate([mine, other], axis=0), jnp.concatenate([other, mine], axis=0)
    )


def on_device(groups, shards, out_grads, hidden_acts, out_basis, in_basis, left_store, right_store, owners):
    per = NQ // groups
    group = lax.axis_index("dp")
    shard = lax.axis_index("mp")
    place = places(owners)
    chunk = per * R
    ring = list(range(0, groups, 2)) + list(range(groups - 1, 0, -2))
    forward = [(ring[i], ring[(i + 1) % groups]) for i in range(groups)]
    backward = [(b, a) for a, b in forward]
    reach = groups // 2

    width_left = left_store.shape[2]
    width_right = right_store.shape[2]
    cut = max(width_right * 5 // 14 // 128 * 128, 128)
    own = [pick_rows(groups, owners, [(left_store, 0, width_left), (right_store, 0, cut)])]
    grads = rotate(out_grads, out_basis, shard)
    own.append(
        pick_rows(groups, after(owners, grads), [(right_store, cut, width_right - cut)])
    )

    steps = [[], []]
    came = []

    def send(piece, hops, others):
        ahead, behind = steps[piece][-1] if hops > 1 else (own[piece], own[piece])
        if hops == reach:
            ahead, behind = ahead[: chunk // 2], behind[chunk // 2 :]
        ahead, behind = after((ahead, behind), others)
        got = (lax.ppermute(ahead, "dp", forward), lax.ppermute(behind, "dp", backward))
        steps[piece].append(got)
        came.append(got)

    def side_by_side(step):
        return jnp.concatenate(step, axis=0)

    acts = rotate(hidden_acts, in_basis, 0)

    for hops in range(1, reach):
        send(0, hops, came[-3:-1])
        send(1, hops, came[-3:-1])
    own_later = after(own, came[0])
    first = [side_by_side(step) for step in steps[0][:-1]] + [own_later[0]]
    second = [side_by_side(step) for step in steps[1][:-1]] + [own_later[1]]
    left_fac = jnp.concatenate([part[:, :width_left] for part in first], axis=0)
    coefficients = [sum_over_shards(contract_rows(grads, left_fac), shards)]
    send(0, reach, came[-3:-1] + coefficients)

    first.append(side_by_side(steps[0][reach - 2]))
    part = contract_rows(grads, first[-1][:, :width_left])
    coefficients.append(small_sum(part, shards, 2))
    send(1, reach, came[-3:-1])

    last = after(steps[0][-1], came[-3])
    second.append(side_by_side(after(steps[1][reach - 2], coefficients[1:2])))
    last = side_by_side(last)
    part = contract_rows(grads, last[:, :width_left]).reshape(-1, LEN, chunk)
    part = jnp.concatenate([part[i] for i in range(part.shape[0])], axis=1)
    last_sum = small_sum(part, shards, 4)
    first.append(after(last, part))
    second.append(side_by_side(steps[1][-1]))
    coefficients.append(last_sum)

    projected = [
        contract_rows(acts[:, :cut], one[:, width_left:]) + contract_rows(acts[:, cut:], other)
        for one, other in zip(first, second)
    ]

    def position(index):
        return jnp.where(index % 2 == 0, index // 2, groups - 1 - index // 2)

    here = position(group)
    row = jnp.arange(chunk, dtype=jnp.int32) // R
    sources = []
    for hops in range(1, reach):
        if hops == reach - 1:
            sources.append((here + 0 * row, row))
        sources += [(here - hops + 0 * row, row), (here + hops + 0 * row, row)]
    half = chunk // 2
    sources += [(here - reach + 0 * row[:half], row[:half]), (here + reach + 0 * row[half:], row[half:])]
    source = jnp.concatenate([s for s, _ in sources]) % groups
    row = jnp.concatenate([r for _, r in sources])
    owner = place // per
    hit = (source[:, None] == position(owner)[None, :]) & (row[:, None] == (place % per)[None, :])
    scores = score(coefficients, projected, hit.astype(jnp.float32))
    return small_sum(scores, shards, 2)


def solution(mesh):
    groups = mesh.shape["dp"]
    shards = mesh.shape["mp"]
    in_specs = (
        P("dp", None),
        P("dp", "mp"),
        P("mp", None, None),
        P("mp", None, None),
        P("dp", None, "mp"),
        P("dp", None, "mp"),
        P(),
    )

    def whole(*arrays):
        return on_device(groups, shards, *arrays)

    return jax.shard_map(
        whole, mesh=mesh, in_specs=in_specs, out_specs=P("dp", None), check_vma=False
    )
```

```python
import jax
import jax.numpy as jnp
from jax import lax
from jax.experimental import pallas as pl
from jax.experimental.pallas import tpu as pltpu
from jax.sharding import PartitionSpec as P

NQ = 16
R = 32
LEN = 128


def params(mebibytes):
    return pltpu.CompilerParams(vmem_limit_bytes=mebibytes * 2**20)


def pick_rows(groups, owners, parts):
    per = NQ // groups
    total = sum(width for _, _, width in parts)

    def kernel(owners_ref, *refs):
        stores, out_ref, sems = refs[:-2], refs[-2], refs[-1]
        group = lax.axis_index("dp")
        found = jnp.int32(0)
        queries = [jnp.int32(0)] * per
        for q in range(NQ):
            own = owners_ref[q] == group
            queries = [jnp.where(own & (found == i), q, at) for i, at in enumerate(queries)]
            found = found + own.astype(jnp.int32)
        copies = []
        for i in range(per):
            rows = pl.ds(pl.multiple_of(queries[i] * R, R), R)
            at = 0
            for j, (store_ref, (_, base, width)) in enumerate(zip(stores, parts)):
                copies.append(
                    pltpu.make_async_copy(
                        store_ref.at[0, rows, pl.ds(base, width)],
                        out_ref.at[pl.ds(i * R, R), pl.ds(at, width)],
                        sems.at[i, j],
                    )
                )
                at += width
        for copy in copies:
            copy.start()
        for copy in copies:
            copy.wait()

    in_hbm = pl.BlockSpec(memory_space=pltpu.HBM)
    return pl.pallas_call(
        kernel,
        out_shape=jax.ShapeDtypeStruct((per * R, total), jnp.bfloat16),
        in_specs=[pl.BlockSpec(memory_space=pltpu.SMEM)] + [in_hbm] * len(parts),
        out_specs=in_hbm,
        scratch_shapes=[pltpu.SemaphoreType.DMA((per, len(parts)))],
        compiler_params=params(52),
        name="pick_rows",
    )(owners, *[store for store, _, _ in parts])


def rotate(matrix, basis, shard):
    rows = matrix.shape[0]
    blocks, width = basis.shape[0], basis.shape[1]
    each = max(n for n in range(1, 5) if blocks % n == 0 and n * width <= 1024)
    steps = blocks // each

    def kernel(shard_ref, matrix_ref, basis_ref, out_ref):
        for k in range(each):
            columns = slice(k * width, (k + 1) * width)
            turned = jnp.dot(
                matrix_ref[:, columns], basis_ref[k], preferred_element_type=jnp.float32
            )
            high = turned.astype(jnp.bfloat16)
            out_ref[:rows, columns] = high
            out_ref[rows:, columns] = (turned - high.astype(jnp.float32)).astype(jnp.bfloat16)

    total = blocks * width
    return pl.pallas_call(
        kernel,
        out_shape=jax.ShapeDtypeStruct((2 * rows, total), jnp.bfloat16),
        grid_spec=pltpu.PrefetchScalarGridSpec(
            num_scalar_prefetch=1,
            grid=(steps,),
            in_specs=[
                pl.BlockSpec((rows, each * width), lambda k, at: (0, at[0] * steps + k)),
                pl.BlockSpec((each, width, width), lambda k, at: (k, 0, 0)),
            ],
            out_specs=pl.BlockSpec((2 * rows, each * width), lambda k, at: (0, k)),
        ),
        compiler_params=params(56),
        cost_estimate=pl.CostEstimate(
            flops=2 * rows * total * width,
            bytes_accessed=2 * (3 * rows * total + total * width),
            transcendentals=0,
        ),
        name="rotate",
    )(jnp.reshape(shard, (1,)).astype(jnp.int32), matrix, basis)


def contract_rows(both, second):
    rows = both.shape[0] // 2
    out = lax.dot_general(
        both, second, (((1,), (1,)), ((), ())), preferred_element_type=jnp.float32
    )
    return out[:rows] + out[rows:]


def score(coefficients, projected, hit):
    sequences = projected[0].shape[0] // LEN
    count = len(coefficients)

    def kernel(hit_ref, *refs):
        out = jnp.zeros((sequences, NQ), jnp.float32)
        at = 0
        which, base = 0, 0
        for part_ref in refs[count:-1]:
            width = part_ref.shape[1]
            if base == refs[which].shape[1]:
                which, base = which + 1, 0
            if which < count - 1:
                terms = (refs[which][:, base : base + width] * part_ref[...]).reshape(sequences, LEN, width)
                base += width
            else:
                terms = jnp.stack(
                    [
                        refs[which][:, i * width : (i + 1) * width] * part_ref[i * LEN : (i + 1) * LEN, :]
                        for i in range(sequences)
                    ]
                )
            out += jnp.dot(
                jnp.sum(terms, axis=1) * (1.0 / LEN),
                hit_ref[at : at + width, :],
                precision=lax.Precision.HIGHEST,
                preferred_element_type=jnp.float32,
            )
            at += width
        refs[-1][...] = out

    return pl.pallas_call(
        kernel,
        out_shape=jax.ShapeDtypeStruct((sequences, NQ), jnp.float32),
        compiler_params=params(32),
        name="score",
    )(hit, *coefficients, *projected)


def places(owners):
    at = jnp.arange(NQ, dtype=jnp.int32)
    before = (owners[None, :] < owners[:, None]) | (
        (owners[None, :] == owners[:, None]) & (at[None, :] < at[:, None])
    )
    return jnp.sum(before.astype(jnp.int32), axis=1)


def swapped(piece, distance, shards):
    return lax.ppermute(piece, "mp", [(i, i ^ distance) for i in range(shards)])


def small_sum(array, shards, most, distance=1):
    while distance < shards:
        reach = min(most, shards // distance)
        array = sum([swapped(array, distance * k, shards) for k in range(1, reach)], array)
        distance *= reach
    return array


def after(value, others):
    return lax.optimization_barrier((value, others))[0] if jax.tree.leaves(others) else value


def sum_over_shards(matrix, shards):
    shard = lax.axis_index("mp")
    bit = shard % 2
    half = matrix.shape[0] // 2
    mine = lax.dynamic_slice_in_dim(matrix, bit * half, half, 0)
    mine = mine + swapped(lax.dynamic_slice_in_dim(matrix, (1 - bit) * half, half, 0), 1, shards)
    mine = small_sum(mine, shards, 2, 2)
    other = swapped(mine, 1, shards)
    return jnp.where(
        bit == 0, jnp.concatenate([mine, other], axis=0), jnp.concatenate([other, mine], axis=0)
    )


def on_device(groups, shards, out_grads, hidden_acts, out_basis, in_basis, left_store, right_store, owners):
    per = NQ // groups
    group = lax.axis_index("dp")
    shard = lax.axis_index("mp")
    place = places(owners)
    chunk = per * R
    ring = list(range(0, groups, 2)) + list(range(groups - 1, 0, -2))
    forward = [(ring[i], ring[(i + 1) % groups]) for i in range(groups)]
    backward = [(b, a) for a, b in forward]
    reach = groups // 2

    width_left = left_store.shape[2]
    width_right = right_store.shape[2]
    cut = max(width_right * 5 // 14 // 128 * 128, 128)
    own = [pick_rows(groups, owners, [(left_store, 0, width_left), (right_store, 0, cut)])]
    grads = rotate(out_grads, out_basis, shard)
    own.append(
        pick_rows(groups, after(owners, grads), [(right_store, cut, width_right - cut)])
    )

    steps = [[], []]
    came = []

    def send(piece, hops, others):
        ahead, behind = steps[piece][-1] if hops > 1 else (own[piece], own[piece])
        if hops == reach:
            ahead, behind = ahead[: chunk // 2], behind[chunk // 2 :]
        ahead, behind = after((ahead, behind), others)
        got = (lax.ppermute(ahead, "dp", forward), lax.ppermute(behind, "dp", backward))
        steps[piece].append(got)
        came.append(got)

    def side_by_side(step):
        return jnp.concatenate(step, axis=0)

    acts = rotate(hidden_acts, in_basis, 0)

    for hops in range(1, reach):
        send(0, hops, came[-3:-1])
        send(1, hops, came[-3:-1])
    own_later = after(own, came[0])
    first = [side_by_side(step) for step in steps[0][:-1]] + [own_later[0]]
    second = [side_by_side(step) for step in steps[1][:-1]] + [own_later[1]]
    left_fac = jnp.concatenate([part[:, :width_left] for part in first], axis=0)
    coefficients = [sum_over_shards(contract_rows(grads, left_fac), shards)]
    send(0, reach, came[-3:-1] + coefficients)

    first.append(side_by_side(steps[0][reach - 2]))
    part = contract_rows(grads, first[-1][:, :width_left])
    coefficients.append(small_sum(part, shards, 2))
    send(1, reach, came[-3:-1])

    last = after(steps[0][-1], came[-3])
    second.append(side_by_side(after(steps[1][reach - 2], coefficients[1:2])))
    last = side_by_side(last)
    part = contract_rows(grads, last[:, :width_left]).reshape(-1, LEN, chunk)
    part = jnp.concatenate([part[i] for i in range(part.shape[0])], axis=1)
    last_sum = small_sum(part, shards, 4)
    first.append(after(last, part))
    second.append(side_by_side(steps[1][-1]))
    coefficients.append(last_sum)

    projected = [
        contract_rows(acts[:, :cut], one[:, width_left:]) + contract_rows(acts[:, cut:], other)
        for one, other in zip(first, second)
    ]

    def position(index):
        return jnp.where(index % 2 == 0, index // 2, groups - 1 - index // 2)

    here = position(group)
    row = jnp.arange(chunk, dtype=jnp.int32) // R
    sources = []
    for hops in range(1, reach):
        if hops == reach - 1:
            sources.append((here + 0 * row, row))
        sources += [(here - hops + 0 * row, row), (here + hops + 0 * row, row)]
    half = chunk // 2
    sources += [(here - reach + 0 * row[:half], row[:half]), (here + reach + 0 * row[half:], row[half:])]
    source = jnp.concatenate([s for s, _ in sources]) % groups
    row = jnp.concatenate([r for _, r in sources])
    owner = place // per
    hit = (source[:, None] == position(owner)[None, :]) & (row[:, None] == (place % per)[None, :])
    scores = score(coefficients, projected, hit.astype(jnp.float32))
    return small_sum(scores, shards, 4)


def solution(mesh):
    groups = mesh.shape["dp"]
    shards = mesh.shape["mp"]
    in_specs = (
        P("dp", None),
        P("dp", "mp"),
        P("mp", None, None),
        P("mp", None, None),
        P("dp", None, "mp"),
        P("dp", None, "mp"),
        P(),
    )

    def whole(*arrays):
        return on_device(groups, shards, *arrays)

    return jax.shard_map(
        whole, mesh=mesh, in_specs=in_specs, out_specs=P("dp", None), check_vma=False
    )
```

```python
import jax
import jax.numpy as jnp
from jax import lax
from jax.experimental import pallas as pl
from jax.experimental.pallas import tpu as pltpu
from jax.sharding import PartitionSpec as P

NQ = 16
R = 32
LEN = 128


def params(mebibytes):
    return pltpu.CompilerParams(vmem_limit_bytes=mebibytes * 2**20)


def pick_rows(groups, owners, parts):
    per = NQ // groups
    total = sum(width for _, _, width in parts)

    def kernel(owners_ref, *refs):
        stores, out_ref, sems = refs[:-2], refs[-2], refs[-1]
        group = lax.axis_index("dp")
        found = jnp.int32(0)
        queries = [jnp.int32(0)] * per
        for q in range(NQ):
            own = owners_ref[q] == group
            queries = [jnp.where(own & (found == i), q, at) for i, at in enumerate(queries)]
            found = found + own.astype(jnp.int32)
        copies = []
        for i in range(per):
            rows = pl.ds(pl.multiple_of(queries[i] * R, R), R)
            at = 0
            for j, (store_ref, (_, base, width)) in enumerate(zip(stores, parts)):
                copies.append(
                    pltpu.make_async_copy(
                        store_ref.at[0, rows, pl.ds(base, width)],
                        out_ref.at[pl.ds(i * R, R), pl.ds(at, width)],
                        sems.at[i, j],
                    )
                )
                at += width
        for copy in copies:
            copy.start()
        for copy in copies:
            copy.wait()

    in_hbm = pl.BlockSpec(memory_space=pltpu.HBM)
    return pl.pallas_call(
        kernel,
        out_shape=jax.ShapeDtypeStruct((per * R, total), jnp.bfloat16),
        in_specs=[pl.BlockSpec(memory_space=pltpu.SMEM)] + [in_hbm] * len(parts),
        out_specs=pl.BlockSpec(memory_space=pltpu.VMEM),
        scratch_shapes=[pltpu.SemaphoreType.DMA((per, len(parts)))],
        compiler_params=params(52),
        name="pick_rows",
    )(owners, *[store for store, _, _ in parts])


def rotate(matrix, basis, shard):
    rows = matrix.shape[0]
    blocks, width = basis.shape[0], basis.shape[1]
    each = max(n for n in range(1, 5) if blocks % n == 0 and n * width <= 1024)
    steps = blocks // each

    def kernel(shard_ref, matrix_ref, basis_ref, out_ref):
        for k in range(each):
            columns = slice(k * width, (k + 1) * width)
            turned = jnp.dot(
                matrix_ref[:, columns], basis_ref[k], preferred_element_type=jnp.float32
            )
            high = turned.astype(jnp.bfloat16)
            out_ref[:rows, columns] = high
            out_ref[rows:, columns] = (turned - high.astype(jnp.float32)).astype(jnp.bfloat16)

    total = blocks * width
    return pl.pallas_call(
        kernel,
        out_shape=jax.ShapeDtypeStruct((2 * rows, total), jnp.bfloat16),
        grid_spec=pltpu.PrefetchScalarGridSpec(
            num_scalar_prefetch=1,
            grid=(steps,),
            in_specs=[
                pl.BlockSpec((rows, each * width), lambda k, at: (0, at[0] * steps + k)),
                pl.BlockSpec((each, width, width), lambda k, at: (k, 0, 0)),
            ],
            out_specs=pl.BlockSpec((2 * rows, each * width), lambda k, at: (0, k)),
        ),
        compiler_params=params(56),
        cost_estimate=pl.CostEstimate(
            flops=2 * rows * total * width,
            bytes_accessed=2 * (3 * rows * total + total * width),
            transcendentals=0,
        ),
        name="rotate",
    )(jnp.reshape(shard, (1,)).astype(jnp.int32), matrix, basis)


def contract_rows(both, second):
    rows = both.shape[0] // 2
    out = lax.dot_general(
        both, second, (((1,), (1,)), ((), ())), preferred_element_type=jnp.float32
    )
    return out[:rows] + out[rows:]


def score(coefficients, projected, hit):
    sequences = projected[0].shape[0] // LEN
    count = len(coefficients)

    def kernel(hit_ref, *refs):
        out = jnp.zeros((sequences, NQ), jnp.float32)
        at = 0
        which, base = 0, 0
        for part_ref in refs[count:-1]:
            width = part_ref.shape[1]
            if base == refs[which].shape[1]:
                which, base = which + 1, 0
            if which < count - 1:
                terms = (refs[which][:, base : base + width] * part_ref[...]).reshape(sequences, LEN, width)
                base += width
            else:
                terms = jnp.stack(
                    [
                        refs[which][:, i * width : (i + 1) * width] * part_ref[i * LEN : (i + 1) * LEN, :]
                        for i in range(sequences)
                    ]
                )
            out += jnp.dot(
                jnp.sum(terms, axis=1) * (1.0 / LEN),
                hit_ref[at : at + width, :],
                precision=lax.Precision.HIGHEST,
                preferred_element_type=jnp.float32,
            )
            at += width
        refs[-1][...] = out

    return pl.pallas_call(
        kernel,
        out_shape=jax.ShapeDtypeStruct((sequences, NQ), jnp.float32),
        compiler_params=params(32),
        name="score",
    )(hit, *coefficients, *projected)


def places(owners):
    at = jnp.arange(NQ, dtype=jnp.int32)
    before = (owners[None, :] < owners[:, None]) | (
        (owners[None, :] == owners[:, None]) & (at[None, :] < at[:, None])
    )
    return jnp.sum(before.astype(jnp.int32), axis=1)


def swapped(piece, distance, shards):
    return lax.ppermute(piece, "mp", [(i, i ^ distance) for i in range(shards)])


def small_sum(array, shards, most, distance=1, others=None):
    while distance < shards:
        reach = min(most, shards // distance)
        copies = [swapped(array, distance * k, shards) for k in range(1, reach)]
        distance *= reach
        array = sum(copies if distance < shards else after(copies, others), array)
    return array


def after(value, others):
    return lax.optimization_barrier((value, others))[0] if jax.tree.leaves(others) else value


def sum_over_shards(matrix, shards):
    shard = lax.axis_index("mp")
    bit = shard % 2
    half = matrix.shape[0] // 2
    mine = lax.dynamic_slice_in_dim(matrix, bit * half, half, 0)
    mine = mine + swapped(lax.dynamic_slice_in_dim(matrix, (1 - bit) * half, half, 0), 1, shards)
    mine = small_sum(mine, shards, 2, 2)
    other = swapped(mine, 1, shards)
    return jnp.where(
        bit == 0, jnp.concatenate([mine, other], axis=0), jnp.concatenate([other, mine], axis=0)
    )


def on_device(groups, shards, out_grads, hidden_acts, out_basis, in_basis, left_store, right_store, owners):
    per = NQ // groups
    group = lax.axis_index("dp")
    shard = lax.axis_index("mp")
    place = places(owners)
    chunk = per * R
    ring = list(range(0, groups, 2)) + list(range(groups - 1, 0, -2))
    forward = [(ring[i], ring[(i + 1) % groups]) for i in range(groups)]
    backward = [(b, a) for a, b in forward]
    reach = groups // 2

    width_left = left_store.shape[2]
    width_right = right_store.shape[2]
    cut = max(width_right * 9 // 28 // 128 * 128, 128)
    own = [pick_rows(groups, owners, [(left_store, 0, width_left), (right_store, 0, cut)])]
    grads = rotate(out_grads, out_basis, shard)
    own.append(
        pick_rows(groups, after(owners, grads), [(right_store, cut, width_right - cut)])
    )

    steps = [[], []]
    came = []

    def send(piece, hops, others):
        ahead, behind = steps[piece][-1] if hops > 1 else (own[piece], own[piece])
        if hops == reach:
            ahead, behind = ahead[: chunk // 2], behind[chunk // 2 :]
        ahead, behind = after((ahead, behind), others)
        got = (lax.ppermute(ahead, "dp", forward), lax.ppermute(behind, "dp", backward))
        steps[piece].append(got)
        came.append(got)

    def side_by_side(step):
        return jnp.concatenate(step, axis=0)

    acts = rotate(hidden_acts, in_basis, 0)

    for hops in range(1, reach):
        send(0, hops, came[-3:-1])
        send(1, hops, came[-3:-1])
    own_later = after(own, came[0])
    first = [side_by_side(step) for step in steps[0][:-1]] + [own_later[0]]
    second = [side_by_side(step) for step in steps[1][:-1]] + [own_later[1]]
    left_fac = jnp.concatenate([part[:, :width_left] for part in first], axis=0)
    coefficients = [sum_over_shards(contract_rows(grads, left_fac), shards)]
    send(0, reach, came[-3:-1] + coefficients)

    first.append(side_by_side(steps[0][reach - 2]))
    part = contract_rows(grads, first[-1][:, :width_left])
    coefficients.append(small_sum(part, shards, 2))
    send(1, reach, came[-3:-1])

    last = after(steps[0][-1], came[-3])
    second.append(side_by_side(after(steps[1][reach - 2], coefficients[1:2])))
    last = side_by_side(last)
    part = contract_rows(grads, last[:, :width_left]).reshape(-1, LEN, chunk)
    part = jnp.concatenate([part[i] for i in range(part.shape[0])], axis=1)
    first.append(after(last, part))
    second.append(side_by_side(steps[1][-1]))

    projected = [
        contract_rows(acts[:, :cut], one[:, width_left:]) + contract_rows(acts[:, cut:], other)
        for one, other in zip(first, second)
    ]

    coefficients.append(small_sum(part, shards, 4, others=projected[-1]))

    def position(index):
        return jnp.where(index % 2 == 0, index // 2, groups - 1 - index // 2)

    here = position(group)
    row = jnp.arange(chunk, dtype=jnp.int32) // R
    sources = []
    for hops in range(1, reach):
        if hops == reach - 1:
            sources.append((here + 0 * row, row))
        sources += [(here - hops + 0 * row, row), (here + hops + 0 * row, row)]
    half = chunk // 2
    sources += [(here - reach + 0 * row[:half], row[:half]), (here + reach + 0 * row[half:], row[half:])]
    source = jnp.concatenate([s for s, _ in sources]) % groups
    row = jnp.concatenate([r for _, r in sources])
    owner = place // per
    hit = (source[:, None] == position(owner)[None, :]) & (row[:, None] == (place % per)[None, :])
    scores = score(coefficients, projected, hit.astype(jnp.float32))
    return small_sum(scores, shards, 4)


def solution(mesh):
    groups = mesh.shape["dp"]
    shards = mesh.shape["mp"]
    in_specs = (
        P("dp", None),
        P("dp", "mp"),
        P("mp", None, None),
        P("mp", None, None),
        P("dp", None, "mp"),
        P("dp", None, "mp"),
        P(),
    )

    def whole(*arrays):
        return on_device(groups, shards, *arrays)

    return jax.shard_map(
        whole, mesh=mesh, in_specs=in_specs, out_specs=P("dp", None), check_vma=False
    )
```

```python
import jax
import jax.numpy as jnp
from jax import lax
from jax.experimental import pallas as pl
from jax.experimental.pallas import tpu as pltpu
from jax.sharding import PartitionSpec as P

NQ = 16
R = 32
LEN = 128


def params(mebibytes):
    return pltpu.CompilerParams(vmem_limit_bytes=mebibytes * 2**20)


def pick_rows(groups, owners, parts):
    per = NQ // groups
    total = sum(width for _, _, width in parts)

    def kernel(owners_ref, *refs):
        stores, out_ref, sems = refs[:-2], refs[-2], refs[-1]
        group = lax.axis_index("dp")
        found = jnp.int32(0)
        queries = [jnp.int32(0)] * per
        for q in range(NQ):
            own = owners_ref[q] == group
            queries = [jnp.where(own & (found == i), q, at) for i, at in enumerate(queries)]
            found = found + own.astype(jnp.int32)
        copies = []
        for i in range(per):
            rows = pl.ds(pl.multiple_of(queries[i] * R, R), R)
            at = 0
            for j, (store_ref, (_, base, width)) in enumerate(zip(stores, parts)):
                copies.append(
                    pltpu.make_async_copy(
                        store_ref.at[0, rows, pl.ds(base, width)],
                        out_ref.at[pl.ds(i * R, R), pl.ds(at, width)],
                        sems.at[i, j],
                    )
                )
                at += width
        for copy in copies:
            copy.start()
        for copy in copies:
            copy.wait()

    in_hbm = pl.BlockSpec(memory_space=pltpu.HBM)
    return pl.pallas_call(
        kernel,
        out_shape=jax.ShapeDtypeStruct((per * R, total), jnp.bfloat16),
        in_specs=[pl.BlockSpec(memory_space=pltpu.SMEM)] + [in_hbm] * len(parts),
        out_specs=pl.BlockSpec(memory_space=pltpu.VMEM),
        scratch_shapes=[pltpu.SemaphoreType.DMA((per, len(parts)))],
        compiler_params=pltpu.CompilerParams(vmem_limit_bytes=54 * 2**20),
        name="pick_rows",
    )(owners, *[store for store, _, _ in parts])


def rotate(matrix, basis, shard):
    rows = matrix.shape[0]
    blocks, width = basis.shape[0], basis.shape[1]
    each = max(n for n in range(1, 5) if blocks % n == 0 and n * width <= 1024)
    steps = blocks // each

    def kernel(shard_ref, matrix_ref, basis_ref, out_ref):
        for k in range(each):
            columns = slice(k * width, (k + 1) * width)
            turned = jnp.dot(
                matrix_ref[:, columns], basis_ref[k], preferred_element_type=jnp.float32
            )
            high = turned.astype(jnp.bfloat16)
            out_ref[:rows, columns] = high
            out_ref[rows:, columns] = (turned - high.astype(jnp.float32)).astype(jnp.bfloat16)

    total = blocks * width
    return pl.pallas_call(
        kernel,
        out_shape=jax.ShapeDtypeStruct((2 * rows, total), jnp.bfloat16),
        grid_spec=pltpu.PrefetchScalarGridSpec(
            num_scalar_prefetch=1,
            grid=(steps,),
            in_specs=[
                pl.BlockSpec((rows, each * width), lambda k, at: (0, at[0] * steps + k)),
                pl.BlockSpec((each, width, width), lambda k, at: (k, 0, 0)),
            ],
            out_specs=pl.BlockSpec((2 * rows, each * width), lambda k, at: (0, k)),
        ),
        compiler_params=params(56),
        cost_estimate=pl.CostEstimate(
            flops=2 * rows * total * width,
            bytes_accessed=2 * (3 * rows * total + total * width),
            transcendentals=0,
        ),
        name="rotate",
    )(jnp.reshape(shard, (1,)).astype(jnp.int32), matrix, basis)


def contract_rows(both, second):
    rows = both.shape[0] // 2
    out = lax.dot_general(
        both, second, (((1,), (1,)), ((), ())), preferred_element_type=jnp.float32
    )
    return out[:rows] + out[rows:]


def score(coefficients, projected, hit):
    sequences = projected[0].shape[0] // LEN
    count = len(coefficients)

    def kernel(hit_ref, *refs):
        out = jnp.zeros((sequences, NQ), jnp.float32)
        at = 0
        which, base = 0, 0
        for part_ref in refs[count:-1]:
            width = part_ref.shape[1]
            if base == refs[which].shape[1]:
                which, base = which + 1, 0
            if which < count - 1:
                terms = (refs[which][:, base : base + width] * part_ref[...]).reshape(sequences, LEN, width)
                base += width
            else:
                terms = jnp.stack(
                    [
                        refs[which][:, i * width : (i + 1) * width] * part_ref[i * LEN : (i + 1) * LEN, :]
                        for i in range(sequences)
                    ]
                )
            out += jnp.dot(
                jnp.sum(terms, axis=1) * (1.0 / LEN),
                hit_ref[at : at + width, :],
                precision=lax.Precision.HIGHEST,
                preferred_element_type=jnp.float32,
            )
            at += width
        refs[-1][...] = out

    return pl.pallas_call(
        kernel,
        out_shape=jax.ShapeDtypeStruct((sequences, NQ), jnp.float32),
        compiler_params=params(32),
        name="score",
    )(hit, *coefficients, *projected)


def places(owners):
    at = jnp.arange(NQ, dtype=jnp.int32)
    before = (owners[None, :] < owners[:, None]) | (
        (owners[None, :] == owners[:, None]) & (at[None, :] < at[:, None])
    )
    return jnp.sum(before.astype(jnp.int32), axis=1)


def swapped(piece, distance, shards):
    return lax.ppermute(piece, "mp", [(i, i ^ distance) for i in range(shards)])


def small_sum(array, shards, most, distance=1, others=None):
    while distance < shards:
        reach = min(most, shards // distance)
        copies = [swapped(array, distance * k, shards) for k in range(1, reach)]
        distance *= reach
        array = sum(copies if distance < shards else after(copies, others), array)
    return array


def after(value, others):
    return lax.optimization_barrier((value, others))[0] if jax.tree.leaves(others) else value


def sum_over_shards(matrix, shards):
    shard = lax.axis_index("mp")
    bit = shard % 2
    half = matrix.shape[0] // 2
    mine = lax.dynamic_slice_in_dim(matrix, bit * half, half, 0)
    mine = mine + swapped(lax.dynamic_slice_in_dim(matrix, (1 - bit) * half, half, 0), 1, shards)
    mine = small_sum(mine, shards, 2, 2)
    other = swapped(mine, 1, shards)
    return jnp.where(
        bit == 0, jnp.concatenate([mine, other], axis=0), jnp.concatenate([other, mine], axis=0)
    )


def on_device(groups, shards, out_grads, hidden_acts, out_basis, in_basis, left_store, right_store, owners):
    per = NQ // groups
    group = lax.axis_index("dp")
    shard = lax.axis_index("mp")
    place = places(owners)
    chunk = per * R
    ring = list(range(0, groups, 2)) + list(range(groups - 1, 0, -2))
    forward = [(ring[i], ring[(i + 1) % groups]) for i in range(groups)]
    backward = [(b, a) for a, b in forward]
    reach = groups // 2

    width_left = left_store.shape[2]
    width_right = right_store.shape[2]
    cut = max(width_right * 9 // 28 // 128 * 128, 128)
    own = [pick_rows(groups, owners, [(left_store, 0, width_left), (right_store, 0, cut)])]
    grads = rotate(out_grads, out_basis, shard)
    own.append(
        pick_rows(groups, after(owners, grads), [(right_store, cut, width_right - cut)])
    )

    steps = [[], []]
    came = []

    def send(piece, hops, others):
        ahead, behind = steps[piece][-1] if hops > 1 else (own[piece], own[piece])
        if hops == reach:
            ahead, behind = ahead[: chunk // 2], behind[chunk // 2 :]
        ahead, behind = after((ahead, behind), others)
        got = (lax.ppermute(ahead, "dp", forward), lax.ppermute(behind, "dp", backward))
        steps[piece].append(got)
        came.append(got)

    def side_by_side(step):
        return jnp.concatenate(step, axis=0)

    acts = rotate(hidden_acts, in_basis, 0)

    for hops in range(1, reach):
        send(0, hops, came[-3:-1])
        send(1, hops, came[-3:-1])
    own_later = after(own, came[0])
    first = [side_by_side(step) for step in steps[0][:-1]] + [own_later[0]]
    second = [side_by_side(step) for step in steps[1][:-1]] + [own_later[1]]
    left_fac = jnp.concatenate([part[:, :width_left] for part in first], axis=0)
    coefficients = [sum_over_shards(contract_rows(grads, left_fac), shards)]
    send(0, reach, came[-3:-1] + coefficients)

    first.append(side_by_side(steps[0][reach - 2]))
    part = contract_rows(grads, first[-1][:, :width_left])
    coefficients.append(small_sum(part, shards, 2))
    send(1, reach, came[-3:-1])

    last = after(steps[0][-1], came[-3])
    second.append(side_by_side(after(steps[1][reach - 2], coefficients[1:2])))
    last = side_by_side(last)
    part = contract_rows(grads, last[:, :width_left]).reshape(-1, LEN, chunk)
    part = jnp.concatenate([part[i] for i in range(part.shape[0])], axis=1)
    first.append(after(last, part))
    second.append(side_by_side(steps[1][-1]))

    projected = [
        contract_rows(acts[:, :cut], one[:, width_left:]) + contract_rows(acts[:, cut:], other)
        for one, other in zip(first, second)
    ]

    coefficients.append(small_sum(part, shards, 4, others=projected[-1]))

    def position(index):
        return jnp.where(index % 2 == 0, index // 2, groups - 1 - index // 2)

    here = position(group)
    row = jnp.arange(chunk, dtype=jnp.int32) // R
    sources = []
    for hops in range(1, reach):
        if hops == reach - 1:
            sources.append((here + 0 * row, row))
        sources += [(here - hops + 0 * row, row), (here + hops + 0 * row, row)]
    half = chunk // 2
    sources += [(here - reach + 0 * row[:half], row[:half]), (here + reach + 0 * row[half:], row[half:])]
    source = jnp.concatenate([s for s, _ in sources]) % groups
    row = jnp.concatenate([r for _, r in sources])
    owner = place // per
    hit = (source[:, None] == position(owner)[None, :]) & (row[:, None] == (place % per)[None, :])
    scores = score(coefficients, projected, hit.astype(jnp.float32))
    return small_sum(scores, shards, 4)


def solution(mesh):
    groups = mesh.shape["dp"]
    shards = mesh.shape["mp"]
    in_specs = (
        P("dp", None),
        P("dp", "mp"),
        P("mp", None, None),
        P("mp", None, None),
        P("dp", None, "mp"),
        P("dp", None, "mp"),
        P(),
    )

    def whole(*arrays):
        return on_device(groups, shards, *arrays)

    return jax.shard_map(
        whole, mesh=mesh, in_specs=in_specs, out_specs=P("dp", None), check_vma=False
    )
```

```python
import jax
import jax.numpy as jnp
from jax import lax
from jax.experimental import pallas as pl
from jax.experimental.pallas import tpu as pltpu
from jax.sharding import PartitionSpec as P

NQ = 16
R = 32
LEN = 128


def params(mebibytes):
    return pltpu.CompilerParams(vmem_limit_bytes=mebibytes * 2**20)


def pick_rows(groups, owners, parts):
    per = NQ // groups
    total = sum(width for _, _, width in parts)

    def kernel(owners_ref, *refs):
        stores, out_ref, sems = refs[:-2], refs[-2], refs[-1]
        group = lax.axis_index("dp")
        found = jnp.int32(0)
        queries = [jnp.int32(0)] * per
        for q in range(NQ):
            own = owners_ref[q] == group
            queries = [jnp.where(own & (found == i), q, at) for i, at in enumerate(queries)]
            found = found + own.astype(jnp.int32)
        copies = []
        for i in range(per):
            rows = pl.ds(pl.multiple_of(queries[i] * R, R), R)
            at = 0
            for j, (store_ref, (_, base, width)) in enumerate(zip(stores, parts)):
                copies.append(
                    pltpu.make_async_copy(
                        store_ref.at[0, rows, pl.ds(base, width)],
                        out_ref.at[pl.ds(i * R, R), pl.ds(at, width)],
                        sems.at[i, j],
                    )
                )
                at += width
        for copy in copies:
            copy.start()
        for copy in copies:
            copy.wait()

    in_hbm = pl.BlockSpec(memory_space=pltpu.HBM)
    return pl.pallas_call(
        kernel,
        out_shape=jax.ShapeDtypeStruct((per * R, total), jnp.bfloat16),
        in_specs=[pl.BlockSpec(memory_space=pltpu.SMEM)] + [in_hbm] * len(parts),
        out_specs=pl.BlockSpec(memory_space=pltpu.VMEM),
        scratch_shapes=[pltpu.SemaphoreType.DMA((per, len(parts)))],
        compiler_params=params(52),
        name="pick_rows",
    )(owners, *[store for store, _, _ in parts])


def rotate(matrix, basis, shard):
    rows = matrix.shape[0]
    blocks, width = basis.shape[0], basis.shape[1]
    each = max(n for n in range(1, 5) if blocks % n == 0 and n * width <= 1024)
    steps = blocks // each

    def kernel(shard_ref, matrix_ref, basis_ref, out_ref):
        for k in range(each):
            columns = slice(k * width, (k + 1) * width)
            turned = jnp.dot(
                matrix_ref[:, columns], basis_ref[k], preferred_element_type=jnp.float32
            )
            high = turned.astype(jnp.bfloat16)
            out_ref[:rows, columns] = high
            out_ref[rows:, columns] = (turned - high.astype(jnp.float32)).astype(jnp.bfloat16)

    total = blocks * width
    return pl.pallas_call(
        kernel,
        out_shape=jax.ShapeDtypeStruct((2 * rows, total), jnp.bfloat16),
        grid_spec=pltpu.PrefetchScalarGridSpec(
            num_scalar_prefetch=1,
            grid=(steps,),
            in_specs=[
                pl.BlockSpec((rows, each * width), lambda k, at: (0, at[0] * steps + k)),
                pl.BlockSpec((each, width, width), lambda k, at: (k, 0, 0)),
            ],
            out_specs=pl.BlockSpec((2 * rows, each * width), lambda k, at: (0, k)),
        ),
        compiler_params=params(56),
        cost_estimate=pl.CostEstimate(
            flops=2 * rows * total * width,
            bytes_accessed=2 * (3 * rows * total + total * width),
            transcendentals=0,
        ),
        name="rotate",
    )(jnp.reshape(shard, (1,)).astype(jnp.int32), matrix, basis)


def contract_rows(both, second):
    rows = both.shape[0] // 2
    out = lax.dot_general(
        both, second, (((1,), (1,)), ((), ())), preferred_element_type=jnp.float32
    )
    return out[:rows] + out[rows:]


def score(coefficients, projected, hit):
    sequences = projected[0].shape[0] // LEN
    count = len(coefficients)

    def kernel(hit_ref, *refs):
        out = jnp.zeros((sequences, NQ), jnp.float32)
        at = 0
        which, base = 0, 0
        for part_ref in refs[count:-1]:
            width = part_ref.shape[1]
            if base == refs[which].shape[1]:
                which, base = which + 1, 0
            if which < count - 1:
                terms = (refs[which][:, base : base + width] * part_ref[...]).reshape(sequences, LEN, width)
                base += width
            else:
                terms = jnp.stack(
                    [
                        refs[which][:, i * width : (i + 1) * width] * part_ref[i * LEN : (i + 1) * LEN, :]
                        for i in range(sequences)
                    ]
                )
            out += jnp.dot(
                jnp.sum(terms, axis=1) * (1.0 / LEN),
                hit_ref[at : at + width, :],
                precision=lax.Precision.HIGHEST,
                preferred_element_type=jnp.float32,
            )
            at += width
        refs[-1][...] = out

    return pl.pallas_call(
        kernel,
        out_shape=jax.ShapeDtypeStruct((sequences, NQ), jnp.float32),
        compiler_params=params(32),
        name="score",
    )(hit, *coefficients, *projected)


def places(owners):
    at = jnp.arange(NQ, dtype=jnp.int32)
    before = (owners[None, :] < owners[:, None]) | (
        (owners[None, :] == owners[:, None]) & (at[None, :] < at[:, None])
    )
    return jnp.sum(before.astype(jnp.int32), axis=1)


def swapped(piece, distance, shards):
    return lax.ppermute(piece, "mp", [(i, i ^ distance) for i in range(shards)])


def small_sum(array, shards, most, distance=1, others=None):
    while distance < shards:
        reach = min(most, shards // distance)
        copies = [swapped(array, distance * k, shards) for k in range(1, reach)]
        distance *= reach
        array = sum(copies if distance < shards else after(copies, others), array)
    return array


def after(value, others):
    return lax.optimization_barrier((value, others))[0] if jax.tree.leaves(others) else value


def sum_over_shards(matrix, shards):
    shard = lax.axis_index("mp")
    bit = shard % 2
    half = matrix.shape[0] // 2
    mine = lax.dynamic_slice_in_dim(matrix, bit * half, half, 0)
    mine = mine + swapped(lax.dynamic_slice_in_dim(matrix, (1 - bit) * half, half, 0), 1, shards)
    mine = small_sum(mine, shards, 2, 2)
    other = swapped(mine, 1, shards)
    return jnp.where(
        bit == 0, jnp.concatenate([mine, other], axis=0), jnp.concatenate([other, mine], axis=0)
    )


def on_device(groups, shards, out_grads, hidden_acts, out_basis, in_basis, left_store, right_store, owners):
    per = NQ // groups
    group = lax.axis_index("dp")
    shard = lax.axis_index("mp")
    place = places(owners)
    chunk = per * R
    ring = list(range(0, groups, 2)) + list(range(groups - 1, 0, -2))
    forward = [(ring[i], ring[(i + 1) % groups]) for i in range(groups)]
    backward = [(b, a) for a, b in forward]
    reach = groups // 2

    width_left = left_store.shape[2]
    width_right = right_store.shape[2]
    cut = max(width_right * 19 // 56 // 128 * 128, 128)
    own = [pick_rows(groups, owners, [(left_store, 0, width_left), (right_store, 0, cut)])]
    grads = rotate(out_grads, out_basis, shard)
    own.append(
        pick_rows(groups, after(owners, grads), [(right_store, cut, width_right - cut)])
    )

    steps = [[], []]
    came = []

    def send(piece, hops, others):
        ahead, behind = steps[piece][-1] if hops > 1 else (own[piece], own[piece])
        if hops == reach:
            ahead, behind = ahead[: chunk // 2], behind[chunk // 2 :]
        ahead, behind = after((ahead, behind), others)
        got = (lax.ppermute(ahead, "dp", forward), lax.ppermute(behind, "dp", backward))
        steps[piece].append(got)
        came.append(got)

    def side_by_side(step):
        return jnp.concatenate(step, axis=0)

    acts = rotate(hidden_acts, in_basis, 0)

    for hops in range(1, reach):
        send(0, hops, came[-3:-1])
        send(1, hops, came[-3:-1])
    own_later = after(own, came[0])
    first = [side_by_side(step) for step in steps[0][:-1]] + [own_later[0]]
    second = [side_by_side(step) for step in steps[1][:-1]] + [own_later[1]]
    left_fac = jnp.concatenate([part[:, :width_left] for part in first], axis=0)
    coefficients = [sum_over_shards(contract_rows(grads, left_fac), shards)]
    send(0, reach, came[-3:-1] + coefficients)

    first.append(side_by_side(steps[0][reach - 2]))
    part = contract_rows(grads, first[-1][:, :width_left])
    coefficients.append(small_sum(part, shards, 2))
    send(1, reach, came[-3:-1])

    last = after(steps[0][-1], came[-3])
    second.append(side_by_side(after(steps[1][reach - 2], coefficients[1:2])))
    last = side_by_side(last)
    part = contract_rows(grads, last[:, :width_left]).reshape(-1, LEN, chunk)
    part = jnp.concatenate([part[i] for i in range(part.shape[0])], axis=1)
    first.append(after(last, part))
    second.append(side_by_side(steps[1][-1]))

    projected = [
        contract_rows(acts[:, :cut], one[:, width_left:]) + contract_rows(acts[:, cut:], other)
        for one, other in zip(first, second)
    ]

    coefficients.append(small_sum(part, shards, 4, others=projected[-1]))

    def position(index):
        return jnp.where(index % 2 == 0, index // 2, groups - 1 - index // 2)

    here = position(group)
    row = jnp.arange(chunk, dtype=jnp.int32) // R
    sources = []
    for hops in range(1, reach):
        if hops == reach - 1:
            sources.append((here + 0 * row, row))
        sources += [(here - hops + 0 * row, row), (here + hops + 0 * row, row)]
    half = chunk // 2
    sources += [(here - reach + 0 * row[:half], row[:half]), (here + reach + 0 * row[half:], row[half:])]
    source = jnp.concatenate([s for s, _ in sources]) % groups
    row = jnp.concatenate([r for _, r in sources])
    owner = place // per
    hit = (source[:, None] == position(owner)[None, :]) & (row[:, None] == (place % per)[None, :])
    scores = score(coefficients, projected, hit.astype(jnp.float32))
    return small_sum(scores, shards, 4)


def solution(mesh):
    groups = mesh.shape["dp"]
    shards = mesh.shape["mp"]
    in_specs = (
        P("dp", None),
        P("dp", "mp"),
        P("mp", None, None),
        P("mp", None, None),
        P("dp", None, "mp"),
        P("dp", None, "mp"),
        P(),
    )

    def whole(*arrays):
        return on_device(groups, shards, *arrays)

    return jax.shard_map(
        whole, mesh=mesh, in_specs=in_specs, out_specs=P("dp", None), check_vma=False
    )
```
